32 devices in a mesh: groups: 2 (over y), seq: 4 (over z), head: 2 (over x), sub: 2 (over core).
Axes of the slice: x: 2, y: 2, z: 4, core: 2. Of those that a mesh axis runs over, the one named last changes fastest.
Arguments:
- wave_pieces: float32 [8, 2, 2, 64, 3072], P(('groups', 'seq'), 'head', 'sub'), parts along dimension 0, may hold values from -6 to 6
- piece_target: int32 [8, 2, 2, 64], P(('groups', 'seq'), 'head', 'sub'), parts along dimension 0, may hold values from -1 to 127, as said below
- utt_lengths: int32 [8], P('groups'), parts along dimension 0, may hold values from 1 to 1088, 2176 in all
- sub_weight: bfloat16 [512, 1536], P(None, 'head'), may hold values from -2 to 2
- sub_bias: bfloat16 [1536], P('head'), may hold values from -4 to 4
- norm_gain: float32 [1536], replicated, may hold values from 0.1 to 1.9
- qkv_weight: bfloat16 [1536, 3, 1536], P(None, None, 'head'), may hold values from -0.21875 to 0.21875
- rel_bias: float32 [24, 543], P('head'), may hold values from -4 to 250
Outputs:
- context: bfloat16 [4352, 1536], P(('groups', 'seq', 'sub'), 'head'), parts along dimension 0
The draws below stay inside these ranges and needn't reach their ends.
There are 2 independent parts, one for each index of `groups`. The reference program is written for one: setup_inputs(seed, part) draws one part's arguments, and reference() takes and returns one part's arrays. A program takes and returns all parts, laid end to end along the dimension named above; an argument that names none is the same for every part. Nothing has to cross between parts.
Inputs may be any that keep to these rules, and one draw needn't show every extreme that they name: `piece_target`: each value is -1 (an empty slot) or s * 32 + p, naming piece p of seq index s for the loader's own head and sub indices. Every piece of every eighth is named by exactly one slot of a loader with the same head and sub indices. A loader names at most 16 pieces of one seq index; in every draw some loaders name exactly 16 pieces of every seq index, so that all their slots are full.
All inputs are finite; a program needn't handle non-finite values.
Results may differ from the reference program's by a relative error of at most 0.006.
Values may be sent and summed in bfloat16 or wider, within the bound.
No kernel may reach another device: no remote copies, remote signals or barrier semaphores. Data moves between devices by JAX's collectives and lax.ppermute only.
A program may use at most 64 MiB of HBM per device.

```python
import math
import jax
import jax.numpy as jnp
import numpy as np
from jax import lax

D = 1536
HEADS = 24
HDIM = 64
MEL = 128
NFFT = 512
HOP = 160
FP = 17
CH = 136
PE = 32
PL = 3072
BINS = 257
CAP = 16
LOAD = 64
HEAVY = 1
HALF_TOK = 272
TOKENS = 2176
UTTS = 4
UTT_MOST = 1088
N_SEQ = 4
N_HEAD = 2
N_SUB = 2


def draw_wave_pieces(key, part):
    key_noise, key_gain = jax.random.split(jax.random.fold_in(key, 3))
    shape = (N_SEQ, N_HEAD, N_SUB, LOAD, PL)
    gains = jnp.exp(jax.random.uniform(key_gain, (N_SEQ, N_HEAD, N_SUB, LOAD, 1), jnp.float32, math.log(0.1), 0.0))
    noise = jnp.clip(jax.random.normal(key_noise, shape, jnp.float32), -6.0, 6.0)
    return (noise * gains).astype(jnp.float32)


def column_plan(key):
    key_heavy, key_extra, key_place, key_order = jax.random.split(key, 4)
    heavy_rank = jax.random.permutation(key_heavy, N_SEQ)
    is_heavy = heavy_rank < HEAVY
    light_total = PE - HEAVY * CAP
    light_loaders = N_SEQ - HEAVY
    light_base = light_total // light_loaders
    light_extra = light_total % light_loaders
    priority = jax.vmap(lambda sub_key: jax.random.permutation(sub_key, N_SEQ))(jax.random.split(key_extra, N_SEQ))
    ahead = (priority[:, None, :] < priority[:, :, None]) & jnp.logical_not(is_heavy)[None, None, :]
    light_rank = jnp.sum(ahead.astype(jnp.int32), axis=2)
    counts = jnp.where(is_heavy[None, :], CAP, light_base + (light_rank < light_extra).astype(jnp.int32))
    offsets = jnp.cumsum(counts, axis=1) - counts
    placement = jax.vmap(lambda sub_key: jax.random.permutation(sub_key, PE))(jax.random.split(key_place, N_SEQ))
    slot_number = jnp.arange(LOAD)
    slot_shard = slot_number // CAP
    slot_rank = slot_number % CAP
    live = slot_rank[None, :] < jnp.transpose(counts)[:, slot_shard]
    order_index = jnp.minimum(jnp.transpose(offsets)[:, slot_shard] + slot_rank[None, :], PE - 1)
    position = placement[slot_shard[None, :], order_index]
    targets = jnp.where(live, slot_shard[None, :] * PE + position, -1)
    shuffles = jax.vmap(lambda sub_key: jax.random.permutation(sub_key, LOAD))(jax.random.split(key_order, N_SEQ))
    return jnp.take_along_axis(targets, shuffles, axis=1).astype(jnp.int32)


def draw_piece_target(key, part):
    column_keys = jax.random.split(jax.random.fold_in(key, 11), N_HEAD * N_SUB)
    per_column = jax.vmap(column_plan)(column_keys)
    return jnp.transpose(per_column.reshape(N_HEAD, N_SUB, N_SEQ, LOAD), (2, 0, 1, 3)).astype(jnp.int32)


def draw_sub_weight(key, part):
    key_values, key_scale = jax.random.split(jax.random.fold_in(key, 7))
    column_scale = jnp.exp(jax.random.uniform(key_scale, (1, D), jnp.float32, math.log(0.3), math.log(3.0)))
    values = jnp.clip(jax.random.normal(key_values, (4 * MEL, D), jnp.float32), -4.0, 4.0)
    return (values * column_scale * (1.0 / math.sqrt(4 * MEL))).astype(jnp.bfloat16)


def draw_rel_bias(key, part):
    width = 4 * CH - 1
    key_values = jax.random.fold_in(key, 5)
    values = jnp.clip(jax.random.normal(key_values, (HEADS, width), jnp.float32), -4.0, 4.0)
    return values.astype(jnp.float32)


def shard_levels(own_key, shape, shards, low, high):
    def one(axis_at, blocks):
        heights = jax.random.uniform(jax.random.fold_in(jax.random.fold_in(own_key, 6), axis_at), (blocks,), jnp.float32, low / len(shards), high / len(shards))
        return jnp.repeat(jnp.exp(heights), shape[axis_at] // blocks).reshape((-1,) + (1,) * (len(shape) - axis_at - 1))

    level = one(*shards[0])
    for cut in shards[1:]:
        level = level * one(*cut)
    return level


def length_profile(amount, total, limit, slope):
    portions = [(1 << 20) // math.isqrt(standing ** slope) + 1 for standing in range(2, amount + 1)]
    rest, given = total - limit - (amount - 1), [1] * (amount - 1)
    while rest > 0:
        free = [i for i in range(amount - 1) if given[i] < limit]
        pool, remaining = sum([portions[i] for i in free]), rest
        for i in free:
            more = min(limit - given[i], max(1, remaining * portions[i] // pool), rest)
            given[i] = given[i] + more
            rest = rest - more
    return np.array([limit] + given)


def ragged(rng, count, total, bound, lean):
    if count == 2:
        one = jax.random.randint(rng, (), max(1, total - bound), min(bound, total - 1) + 1)
        return jnp.stack([one, total - one])
    sizes = jnp.asarray(length_profile(count, total, bound, lean), jnp.int32)
    twos = (count - 1) // 2
    source_of, taker = sizes[1:1 + 2 * twos:2], sizes[2:2 + 2 * twos:2]
    margin = jnp.minimum(source_of - 1, bound - taker)
    shifted = jax.random.randint(jax.random.fold_in(rng, 1), (twos,), 0, 1 << 20) % (margin + 1)
    sizes = sizes.at[1:1 + 2 * twos:2].set(source_of - shifted).at[2:2 + 2 * twos:2].set(taker + shifted)
    return sizes[jax.random.permutation(jax.random.fold_in(rng, 2), count)]


def normal_values(key, dims, deviation, bound, pieces=(), held_as=jnp.bfloat16):
    array = deviation * jax.random.normal(key, dims, jnp.float32)
    if pieces:
        array = array * shard_levels(key, dims, pieces, -0.22, 0.18)
    return jnp.clip(array, -bound, bound).astype(held_as)


def setup_inputs(seed: int = 0, part: int = 0) -> dict:
    arg_keys = jax.random.split(jax.random.key(seed), 9)
    part_keys = jax.random.split(jax.random.fold_in(arg_keys[8], part), 9)
    wave_pieces = draw_wave_pieces(jax.random.fold_in(jax.random.fold_in(arg_keys[8], part), 71), part)
    piece_target = draw_piece_target(jax.random.fold_in(jax.random.fold_in(arg_keys[8], part), 71), part)
    utt_lengths = ragged(part_keys[2], UTTS, TOKENS, UTT_MOST, 2).astype(jnp.int32)
    sub_weight = draw_sub_weight(jax.random.fold_in(arg_keys[8], 71), part)
    sub_bias = normal_values(arg_keys[4], (D,), 1.0, 4.0, ((0, 2),))
    norm_gain = jnp.clip(1.0 + 0.18 * jax.random.normal(arg_keys[5], (D,), jnp.float32), 0.1, 1.9)
    qkv_weight = normal_values(arg_keys[6], (D, 3, D), (D // 2) ** -0.5, 0.21875, ((2, 2),))
    rel_bias = draw_rel_bias(jax.random.fold_in(arg_keys[8], 71), part)
    return {"wave_pieces": wave_pieces, "piece_target": piece_target, "utt_lengths": utt_lengths, "sub_weight": sub_weight, "sub_bias": sub_bias, "norm_gain": norm_gain, "qkv_weight": qkv_weight, "rel_bias": rel_bias}


SAMPLE_RATE = 16000.0
EPSILON = 1e-05
MASKED = -1e+30

def window_table():
    sample_index = jnp.arange(NFFT).astype(jnp.float32)
    return 0.5 - 0.5 * jnp.cos(2.0 * math.pi / NFFT * sample_index)

def fourier_table():
    sample_index = jnp.arange(NFFT).astype(jnp.int32)[:, None]
    bin_index = jnp.arange(BINS).astype(jnp.int32)[None, :]
    phase = (sample_index * bin_index % NFFT).astype(jnp.float32) * (2.0 * math.pi / NFFT)
    return jnp.concatenate([jnp.cos(phase), jnp.sin(phase)], axis=1)

def mel_table():
    highest = 2595.0 * math.log10(1.0 + SAMPLE_RATE / 2.0 / 700.0)
    points = jnp.arange(MEL + 2).astype(jnp.float32) * (highest / (MEL + 1))
    hertz = 700.0 * (jnp.power(10.0, points / 2595.0) - 1.0)
    centres = jnp.arange(BINS).astype(jnp.float32) * (SAMPLE_RATE / NFFT)
    rising = (centres[:, None] - hertz[None, :-2]) / (hertz[1:-1] - hertz[:-2])[None, :]
    falling = (hertz[None, 2:] - centres[:, None]) / (hertz[2:] - hertz[1:-1])[None, :]
    return jnp.maximum(0.0, jnp.minimum(rising, falling))

def log_mel(piece_rows):
    piece_count = piece_rows.shape[0]
    frames = jnp.stack([piece_rows[:, HOP * frame_index:HOP * frame_index + NFFT] for frame_index in range(FP)], axis=1)
    frames = frames * window_table()[None, None, :]
    spectra = jnp.dot(frames.reshape(piece_count * FP, NFFT), fourier_table(), precision=lax.Precision.HIGHEST)
    power_bins = spectra[:, :BINS] * spectra[:, :BINS] + spectra[:, BINS:] * spectra[:, BINS:]
    energy = jnp.dot(power_bins, mel_table(), precision=lax.Precision.HIGHEST)
    return jnp.log(1.0 + energy).astype(jnp.bfloat16).reshape(piece_count, FP * MEL)

def reference(wave_pieces, piece_target, utt_lengths, sub_weight, sub_bias, norm_gain, qkv_weight, rel_bias):
    column_count = N_HEAD * N_SUB
    slot_rows = jnp.transpose(wave_pieces, (1, 2, 0, 3, 4)).reshape(column_count, N_SEQ * LOAD, PL)
    targets = jnp.transpose(piece_target, (1, 2, 0, 3)).reshape(column_count, N_SEQ * LOAD).astype(jnp.int32)
    targets = jnp.where(targets < 0, N_SEQ * PE, targets).astype(jnp.int32)

    def place(column_rows, slot_goals):
        return jnp.zeros((N_SEQ * PE, PL), jnp.float32).at[slot_goals].set(column_rows.astype(jnp.float32), mode='drop')
    placed = jax.vmap(place)(slot_rows, targets)
    placed = jnp.transpose(placed.reshape(N_HEAD, N_SUB, N_SEQ, PE, PL), (2, 1, 0, 3, 4))

    def shard_mel(shard_pieces):
        return log_mel(shard_pieces.reshape(N_SUB * N_HEAD * PE, PL))
    mel_pieces = lax.map(shard_mel, placed)
    token_rows = mel_pieces.reshape(TOKENS, 4 * MEL)
    features = jax.nn.silu(jnp.dot(token_rows, sub_weight, preferred_element_type=jnp.float32) + sub_bias.astype(jnp.float32)).astype(jnp.bfloat16)

    def project(half_rows):
        values = half_rows.astype(jnp.float32)
        centred = values - lax.optimization_barrier(jnp.mean(values, axis=1, keepdims=True))
        variance = lax.optimization_barrier(jnp.mean(centred * centred, axis=1, keepdims=True))
        normed = (centred * lax.rsqrt(variance + EPSILON) * norm_gain[None, :]).astype(jnp.bfloat16)
        return jnp.dot(normed, qkv_weight.reshape(D, 3 * D), preferred_element_type=jnp.float32).astype(jnp.bfloat16)
    projected = lax.map(project, features.reshape(N_SEQ * N_SUB, HALF_TOK, D)).reshape(TOKENS, 3, HEADS, HDIM)
    queries = projected[:, 0]
    padding = jnp.zeros((CH, HEADS, HDIM), jnp.bfloat16)
    key_padded = jnp.concatenate([padding, projected[:, 1], padding], axis=0)
    value_padded = jnp.concatenate([padding, projected[:, 2], padding], axis=0)
    utterance_ends = jnp.cumsum(utt_lengths).astype(jnp.int32)
    positions = (jnp.arange(TOKENS + 2 * CH) - CH).astype(jnp.int32)
    utterance_ids = lax.optimization_barrier(jnp.sum((utterance_ends[None, :] <= positions[:, None]).astype(jnp.int32), axis=1)).astype(jnp.int32)
    key_inside = (positions >= 0) & (positions < TOKENS)
    relative_index = (jnp.arange(CH)[:, None] - jnp.arange(3 * CH)[None, :] + 3 * CH - 1).astype(jnp.int32)
    position_bias = rel_bias[:, relative_index]

    def attend(block_index):
        start = (block_index * CH).astype(jnp.int32)
        query_block = lax.dynamic_slice_in_dim(queries, start, CH, 0).astype(jnp.float32)
        key_block = lax.dynamic_slice_in_dim(key_padded, start, 3 * CH, 0).astype(jnp.float32)
        value_block = lax.dynamic_slice_in_dim(value_padded, start, 3 * CH, 0).astype(jnp.float32)
        query_utt = lax.dynamic_slice_in_dim(utterance_ids, start + CH, CH, 0)
        key_utt = lax.dynamic_slice_in_dim(utterance_ids, start, 3 * CH, 0)
        key_valid = lax.dynamic_slice_in_dim(key_inside, start, 3 * CH, 0)
        scores = jnp.einsum('qhd,khd->hqk', query_block, key_block) * (1.0 / math.sqrt(HDIM)) + position_bias
        allowed = (query_utt[:, None] == key_utt[None, :]) & key_valid[None, :]
        scores = jnp.where(allowed[None, :, :], scores, MASKED)
        row_peak = lax.optimization_barrier(jnp.max(scores, axis=2, keepdims=True))
        weights = jnp.exp(scores - row_peak)
        attention_weights = (weights / lax.optimization_barrier(jnp.sum(weights, axis=2, keepdims=True))).astype(jnp.bfloat16)
        context = jnp.einsum('hqk,khd->qhd', attention_weights.astype(jnp.float32), value_block)
        return context.astype(jnp.bfloat16).reshape(CH, D)
    contexts = lax.map(attend, jnp.arange(TOKENS // CH).astype(jnp.int32))
    return contexts.reshape(TOKENS, D)
```

```python
import functools
import math

import jax
import jax.numpy as jnp
import ml_dtypes
import numpy as np
from jax import lax
from jax.experimental import pallas as pl
from jax.experimental.pallas import tpu as pltpu
from jax.sharding import PartitionSpec as P

HDIM = 64
MEL = 128
NFFT = 512
HOP = 160
FP = 17
CH = 136
PE = 32

SAMPLE_RATE = 16000.0
EPSILON = 1e-05
MASKED = -1e30

LANES = 128
PIECE_BITS = 5
ROWS = 144
GROUP = 4
STACK = 4
MEL_WIDTH = FP * MEL
BF16 = jnp.bfloat16
F32 = jnp.float32


def split_bf16(values):
    high = values.astype(ml_dtypes.bfloat16)
    low = (values - high.astype(np.float64)).astype(ml_dtypes.bfloat16)
    return np.stack([high, low])


def fourier_tables():
    n = np.arange(NFFT)
    bins = NFFT // 2
    window = 0.5 - 0.5 * np.cos(2.0 * np.pi * n / NFFT)
    phase = 2.0 * np.pi * ((n[:, None] * np.arange(bins + 1)[None, :]) % NFFT) / NFFT
    sine = np.sin(phase[:, :bins])
    sine[:, 0] = np.cos(phase[:, bins])
    return split_bf16(np.concatenate([np.cos(phase[:, :bins]), sine], axis=1) * window[:, None])


def mel_tables():
    bins = NFFT // 2
    highest = 2595.0 * math.log10(1.0 + SAMPLE_RATE / 2.0 / 700.0)
    points = np.arange(MEL + 2) * (highest / (MEL + 1))
    hertz = 700.0 * (10.0 ** (points / 2595.0) - 1.0)
    centres = np.arange(bins + 1) * (SAMPLE_RATE / NFFT)
    rising = (centres[:, None] - hertz[None, :-2]) / (hertz[1:-1] - hertz[:-2])[None, :]
    falling = (hertz[None, 2:] - centres[:, None]) / (hertz[2:] - hertz[1:-1])[None, :]
    filters = np.maximum(0.0, np.minimum(rising, falling))
    second = filters[:bins].copy()
    second[0] = filters[bins]
    return split_bf16(np.concatenate([filters[:bins], second], axis=0))


def dot(a, b):
    return jnp.dot(a, b, preferred_element_type=F32)


def iota(shape, dim):
    return lax.broadcasted_iota(jnp.int32, shape, dim)


def mel_kernel(shards, capacity, relative, x_ref, target_ref, fourier_ref, mel_ref, *outs):
    slots = x_ref.shape[0]
    x = x_ref[...]
    frames = [None] * FP
    for phase in range(4):
        shift = phase * (HOP % LANES)
        moved = x if phase == 0 else pltpu.roll(x, x.shape[1] - shift, 1)
        high = moved.astype(BF16)
        low = (moved - high.astype(F32)).astype(BF16)
        members = list(range(phase, FP, 4))
        starts = [HOP * f - shift for f in members]
        high = jnp.concatenate([high[:, s : s + NFFT] for s in starts], axis=0)
        low = jnp.concatenate([low[:, s : s + NFFT] for s in starts], axis=0)
        spectra = dot(high, fourier_ref[0]) + dot(low, fourier_ref[0]) + dot(high, fourier_ref[1])
        power = spectra * spectra
        power_high = power.astype(BF16)
        power_low = (power - power_high.astype(F32)).astype(BF16)
        energy = (
            dot(power_high, mel_ref[0]) + dot(power_low, mel_ref[0]) + dot(power_high, mel_ref[1])
        )
        log_mel = jnp.log(1.0 + energy).astype(BF16)
        for k, f in enumerate(members):
            frames[f] = log_mel[k * slots : (k + 1) * slots]
    target = target_ref[...]
    owner = lax.shift_right_arithmetic(target, PIECE_BITS)
    place = jnp.where(target < 0, 0, (target & (PE - 1)) + 1).astype(F32)
    row, col = iota((slots, slots), 0), iota((slots, slots), 1)
    diagonal = row == col
    owner_col = jnp.sum(jnp.where(diagonal, owner, 0), axis=1, keepdims=True)
    place_col = jnp.sum(jnp.where(diagonal, place, 0.0), axis=1, keepdims=True)
    rank = jnp.sum(((owner_col == owner) & (row < col)).astype(jnp.int32), axis=0, keepdims=True)
    chosen = row // capacity
    if relative:
        chosen = chosen ^ lax.axis_index("seq")
    pick = ((chosen == owner) & (row % capacity == rank)).astype(F32).astype(BF16)
    marks = jnp.broadcast_to(place_col, (slots, LANES)).astype(BF16)
    packed = dot(pick, jnp.concatenate(frames + [marks], axis=1)).astype(BF16)
    count = slots // len(outs)
    for d, out in enumerate(outs):
        out[...] = packed[d * count : (d + 1) * count]


def place_kernel(*refs):
    parts, out = refs[:-1], refs[-1]
    rows = jnp.concatenate([part[...] for part in parts], axis=0)
    slots = rows.shape[0]
    mark = rows[:, MEL_WIDTH : MEL_WIDTH + LANES].astype(F32)[:, :1]
    row, col = iota((slots, slots), 0), iota((slots, slots), 1)
    mark = jnp.sum(jnp.where(row == col, mark, 0.0), axis=0, keepdims=True)
    at = iota((PE, slots), 0)
    groups = PE // GROUP
    wanted = (at % groups) * GROUP + at // groups + 1
    pick = (wanted.astype(F32) == mark).astype(F32).astype(BF16)
    out[...] = dot(pick, rows[:, :MEL_WIDTH]).astype(BF16)


def token_rows(pieces):
    groups = PE // GROUP
    pieces = pieces.astype(F32)
    rows = []
    for i in range(FP):
        cells = []
        for j in range(STACK):
            q, f = divmod(STACK * i + j, FP)
            cells.append(pieces[q * groups : (q + 1) * groups, f * MEL : (f + 1) * MEL])
        rows.append(jnp.concatenate(cells, axis=1))
    rows.append(jnp.zeros((ROWS - CH, STACK * MEL), F32))
    mixed = jnp.concatenate(rows, axis=0).astype(BF16)
    row, col = iota((ROWS, ROWS), 0), iota((ROWS, ROWS), 1)
    token = (col % groups) * FP + col // groups
    order = ((row == token) & (col < CH)).astype(F32).astype(BF16)
    return dot(order, mixed).astype(BF16)


def bias_kernel(lengths_ref, table_ref, out_ref):
    pairs, blocks = out_ref.shape[:2]
    half = blocks * CH
    first = (lax.axis_index("seq") * lax.axis_size("sub") + lax.axis_index("sub")) * half
    total = lax.axis_size("seq") * lax.axis_size("sub") * half
    lane, row = iota((1, 3 * ROWS), 1), iota((ROWS, 1), 0)
    key_block = lane // ROWS
    key_place = lane - key_block * ROWS
    masks = []
    for c in range(blocks):
        query = first + c * CH + row
        key = first + (c - 1) * CH + key_block * CH + key_place
        query_utt, key_utt = jnp.zeros_like(query), jnp.zeros_like(key)
        end = jnp.int32(0)
        for r in range(lengths_ref.shape[0]):
            end = end + lengths_ref[r]
            query_utt = query_utt + (query >= end).astype(jnp.int32)
            key_utt = key_utt + (key >= end).astype(jnp.int32)
        inside = (key >= 0) & (key < total) & (key_place < CH)
        key_utt = jnp.where(inside, key_utt, -1)
        masks.append(jnp.where(query_utt == key_utt, 0.0, MASKED))
    width = table_ref.shape[1]

    def one_head(head, side):
        line = jnp.broadcast_to(table_ref[pl.ds(head, 1), :], (ROWS, width))
        turned = [
            pltpu.roll(line, (8 * b - (CH - 1)) % width, 1, stride=1, stride_axis=0)[:, : 3 * ROWS]
            for b in range(3)
        ]
        bias = jnp.where(
            key_block == 0, turned[0], jnp.where(key_block == 1, turned[1], turned[2])
        )
        for c in range(blocks):
            out_ref[head // 2, c, side * ROWS : (side + 1) * ROWS, :] = bias + masks[c]

    @pl.loop(0, pairs)
    def _(pair):
        one_head(2 * pair, 0)
        one_head(2 * pair + 1, 1)


def attend_kernel(heads_split, *refs):
    n = heads_split
    pieces, refs = refs[: n + 2], refs[n + 2 :]
    conv, refs = refs[: 1 + 2 * (n - 1)], refs[1 + 2 * (n - 1) :]
    conv_bias, gain, qkv_hbm, bias_hbm, out = refs[:5]
    tokens, normed, queries, keys, values, qkv, bias, sems = refs[5:]
    me = lax.axis_index("head")
    depth = qkv.shape[1] // n
    copies = []
    for p in range(3):
        for d in range(n):
            source = pl.multiple_of(lax.rem(me + d, n) * depth, depth)
            copy = pltpu.make_async_copy(
                qkv_hbm.at[p, pl.ds(source, depth), :],
                qkv.at[p, pl.ds(d * depth, depth), :],
                sems.at[p * n + d],
            )
            copy.start()
            copies.append(copy)
    bias_copy = pltpu.make_async_copy(bias_hbm, bias, sems.at[3 * n])
    bias_copy.start()

    blocks = n + 2
    tokens[0] = token_rows(pieces[n][...])
    tokens[n + 1] = token_rows(pieces[n + 1][...])
    for d in range(n):
        tokens[1 + lax.rem(me + d, n)] = token_rows(pieces[d][...])
    every = tokens[...].reshape(blocks * ROWS, STACK * MEL)
    features = []
    for d in range(n):
        if d == 0:
            summed = dot(every, conv[0][...])
        else:
            rows = conv[2 * d - 1].shape[0]
            summed = dot(every[:, :rows], conv[2 * d - 1][...])
            summed = summed + dot(every[:, rows:], conv[2 * d][...])
        summed = summed + conv_bias[d].astype(F32)
        features.append((summed / (1.0 + jnp.exp(-summed))).astype(BF16).astype(F32))
    width = depth * n
    mean = sum(jnp.sum(f, axis=1, keepdims=True) for f in features) * (1.0 / width)
    centred = [f - mean for f in features]
    variance = sum(jnp.sum(c * c, axis=1, keepdims=True) for c in centred) * (1.0 / width)
    scale = lax.rsqrt(variance + EPSILON)
    for d in range(n):
        normed[:, d * depth : (d + 1) * depth] = (
            centred[d] * scale * gain[lax.rem(me + d, n)]
        ).astype(BF16)

    for copy in copies:
        copy.wait()
    local = qkv.shape[2]
    queries[...] = dot(normed[ROWS : (n + 1) * ROWS, :], qkv[0]).astype(BF16).reshape(
        n, ROWS, local
    )
    keys[...] = dot(normed[...], qkv[1]).astype(BF16).reshape(blocks, ROWS, local)
    values[...] = dot(normed[...], qkv[2]).astype(BF16).reshape(blocks, ROWS, local)
    bias_copy.wait()
    lane = iota((ROWS, LANES), 1)
    low_lanes = lane < HDIM

    @pl.loop(0, local // LANES)
    def _(pair):
        at = pl.ds(pl.multiple_of(pair * LANES, LANES), LANES)
        results = []
        for c in range(n):
            q = queries[c, :, at] * jnp.asarray(1.0 / math.sqrt(HDIM), BF16)
            zero = jnp.zeros_like(q)
            q = jnp.concatenate(
                [jnp.where(low_lanes, q, zero), jnp.where(low_lanes, zero, q)], axis=0
            )
            k = keys[c : c + 3, :, at].reshape(3 * ROWS, LANES)
            v = values[c : c + 3, :, at].reshape(3 * ROWS, LANES)
            scores = lax.dot_general(q, k, (((1,), (1,)), ((), ())), preferred_element_type=F32)
            scores = scores + bias[pair, c]
            weights = jnp.exp(scores - jnp.max(scores, axis=1, keepdims=True))
            weights = weights / jnp.sum(weights, axis=1, keepdims=True)
            context = dot(weights.astype(BF16), v)
            results.append(jnp.where(low_lanes, context[:ROWS], context[ROWS:])[:CH])
        out[:, at] = jnp.concatenate(results, axis=0).astype(BF16)


def vmem(count):
    return [pl.BlockSpec(memory_space=pltpu.VMEM)] * count


def exchange_weights(weight):
    n, cores = lax.axis_size("head"), lax.axis_size("sub")
    assert cores == 2
    rows = weight.shape[0] // cores
    core = lax.axis_index("sub")
    mine = lax.dynamic_slice_in_dim(weight, core * rows, rows, 0)
    pieces = []
    for d in range(1, n):
        got = lax.ppermute(mine, "head", [((i + d) % n, i) for i in range(n)])
        swapped = lax.ppermute(got, "sub", [(0, 1), (1, 0)])
        pieces.append(jnp.where(core == 0, got, swapped))
        pieces.append(jnp.where(core == 0, swapped, got))
    return pieces


def local(
    wave_pieces, piece_target, utt_lengths, sub_weight, sub_bias, norm_gain, qkv_weight, rel_bias
):
    shards, n, cores = lax.axis_size("seq"), lax.axis_size("head"), lax.axis_size("sub")
    slots, length = wave_pieces.shape[3:]
    capacity = slots // shards
    relative = shards in (2, 4) and capacity % 16 == 0
    outs = shards if relative else 1
    payload = MEL_WIDTH + LANES
    packed = pl.pallas_call(
        functools.partial(mel_kernel, shards, capacity, relative),
        out_shape=[jax.ShapeDtypeStruct((slots // outs, payload), BF16)] * outs,
        in_specs=vmem(4),
        out_specs=vmem(outs),
        compiler_params=pltpu.CompilerParams(vmem_limit_bytes=40 << 20),
        name="log_mel",
    )(
        wave_pieces.reshape(slots, length),
        piece_target.reshape(1, slots),
        jnp.asarray(fourier_tables()),
        jnp.asarray(mel_tables()),
    )
    if relative:
        received = [packed[0]] + [
            lax.ppermute(packed[d], "seq", [(i, i ^ d) for i in range(shards)])
            for d in range(1, shards)
        ]
    else:
        blocks = packed[0].reshape(shards, capacity, payload)
        blocks = lax.all_to_all(blocks, "seq", split_axis=0, concat_axis=0, tiled=True)
        received = [blocks.reshape(slots, payload)]
    own = pl.pallas_call(
        place_kernel,
        out_shape=jax.ShapeDtypeStruct((PE, MEL_WIDTH), BF16),
        in_specs=vmem(len(received)),
        out_specs=vmem(1)[0],
        name="place",
    )(*received)

    halves = shards * cores
    axes = ("seq", "head", "sub")

    def device(half, head):
        return ((half // cores) * n + head) * cores + half % cores

    others = [
        lax.ppermute(own, "head", [((i + d) % n, i) for i in range(n)]) for d in range(1, n)
    ]
    around = []
    for d in range(n):
        pairs = []
        for half in range(halves - 1):
            pairs.append((device(half, n - 1), device(half + 1, d)))
            pairs.append((device(half + 1, 0), device(half, (d + 1) % n)))
        around.append(lax.ppermute(own, axes, pairs))
    me = lax.axis_index("head")
    previous, following = around[0], around[n - 1]
    for d in range(1, n):
        previous = jnp.where(me == d, around[d], previous)
        following = jnp.where(me == d, around[d - 1], following)

    local_width = qkv_weight.shape[2]
    pairs = local_width // LANES
    table = jnp.pad(rel_bias[:, ::-1], ((0, 0), (0, -rel_bias.shape[1] % LANES)))
    bias = pl.pallas_call(
        bias_kernel,
        out_shape=jax.ShapeDtypeStruct((pairs, n, 2 * ROWS, 3 * ROWS), F32),
        in_specs=[pl.BlockSpec(memory_space=pltpu.SMEM), pl.BlockSpec(memory_space=pltpu.VMEM)],
        out_specs=vmem(1)[0],
        compiler_params=pltpu.CompilerParams(vmem_limit_bytes=40 << 20),
        name="bias",
    )(utt_lengths, table)
    conv = [sub_weight] + exchange_weights(sub_weight)
    conv_bias = jnp.stack(
        [sub_bias]
        + [
            lax.ppermute(sub_bias, "head", [((i + d) % n, i) for i in range(n)])
            for d in range(1, n)
        ]
    )
    conv_bias = conv_bias.reshape(n, 1, sub_bias.shape[0])
    width = qkv_weight.shape[0]
    blocks = n + 2
    return pl.pallas_call(
        functools.partial(attend_kernel, n),
        out_shape=jax.ShapeDtypeStruct((n * CH, local_width), BF16),
        in_specs=vmem(blocks + len(conv) + 2) + [pl.BlockSpec(memory_space=pl.ANY)] * 2,
        out_specs=vmem(1)[0],
        scratch_shapes=[
            pltpu.VMEM((blocks, ROWS, STACK * MEL), BF16),
            pltpu.VMEM((blocks * ROWS, width), BF16),
            pltpu.VMEM((n, ROWS, local_width), BF16),
            pltpu.VMEM((blocks, ROWS, local_width), BF16),
            pltpu.VMEM((blocks, ROWS, local_width), BF16),
            pltpu.VMEM((3, width, local_width), BF16),
            pltpu.VMEM(bias.shape, F32),
            pltpu.SemaphoreType.DMA((3 * n + 1,)),
        ],
        compiler_params=pltpu.CompilerParams(vmem_limit_bytes=48 << 20),
        name="attend",
    )(
        own,
        *others,
        previous,
        following,
        *conv,
        conv_bias,
        norm_gain.reshape(n, 1, width // n),
        jnp.transpose(qkv_weight, (1, 0, 2)),
        bias,
    )


def solution(mesh):
    placed = (
        P(("groups", "seq"), "head", "sub", None, None),
        P(("groups", "seq"), "head", "sub", None),
        P("groups"),
        P(None, "head"),
        P("head"),
        P(),
        P(None, None, "head"),
        P("head", None),
    )
    return jax.shard_map(
        local,
        mesh=mesh,
        in_specs=placed,
        out_specs=P(("groups", "seq", "sub"), "head"),
        check_vma=False,
    )
```

```python
import functools
import math

import jax
import jax.numpy as jnp
import ml_dtypes
import numpy as np
from jax import lax
from jax.experimental import pallas as pl
from jax.experimental.pallas import tpu as pltpu
from jax.sharding import PartitionSpec as P

HDIM = 64
MEL = 128
NFFT = 512
HOP = 160
FP = 17
CH = 136
PE = 32

SAMPLE_RATE = 16000.0
EPSILON = 1e-05
MASKED = -1e30

LANES = 128
PIECE_BITS = 5
ROWS = 144
GROUP = 4
STACK = 4
MEL_WIDTH = FP * MEL
BF16 = jnp.bfloat16
F32 = jnp.float32


def split_bf16(values):
    high = values.astype(ml_dtypes.bfloat16)
    low = (values - high.astype(np.float64)).astype(ml_dtypes.bfloat16)
    return np.stack([high, low])


def fourier_tables():
    n = np.arange(NFFT)
    bins = NFFT // 2
    window = 0.5 - 0.5 * np.cos(2.0 * np.pi * n / NFFT)
    phase = 2.0 * np.pi * ((n[:, None] * np.arange(bins + 1)[None, :]) % NFFT) / NFFT
    sine = np.sin(phase[:, :bins])
    sine[:, 0] = np.cos(phase[:, bins])
    return split_bf16(np.concatenate([np.cos(phase[:, :bins]), sine], axis=1) * window[:, None])


def mel_tables():
    bins = NFFT // 2
    highest = 2595.0 * math.log10(1.0 + SAMPLE_RATE / 2.0 / 700.0)
    points = np.arange(MEL + 2) * (highest / (MEL + 1))
    hertz = 700.0 * (10.0 ** (points / 2595.0) - 1.0)
    centres = np.arange(bins + 1) * (SAMPLE_RATE / NFFT)
    rising = (centres[:, None] - hertz[None, :-2]) / (hertz[1:-1] - hertz[:-2])[None, :]
    falling = (hertz[None, 2:] - centres[:, None]) / (hertz[2:] - hertz[1:-1])[None, :]
    filters = np.maximum(0.0, np.minimum(rising, falling))
    high, low = split_bf16(np.concatenate([filters, np.zeros((15, MEL))], axis=0))
    return np.concatenate([high, low], axis=1)


def dot(a, b):
    return jnp.dot(a, b, preferred_element_type=F32)


def iota(shape, dim):
    return lax.broadcasted_iota(jnp.int32, shape, dim)


def mel_kernel(
    shards, capacity, relative, x_hbm, target_hbm, weight_hbm, fourier_hbm, mel_hbm, *refs
):
    sent, *outs = refs[:-5]
    x_ref, target_ref, fourier_ref, mel_ref, sems = refs[-5:]
    slots, rows = x_ref.shape[0], sent.shape[0]
    first = pl.multiple_of(lax.axis_index("sub") * rows, rows)
    copies = [
        pltpu.make_async_copy(source, target, sems.at[k])
        for k, (source, target) in enumerate(
            (
                (x_hbm, x_ref),
                (fourier_hbm, fourier_ref),
                (mel_hbm, mel_ref),
                (target_hbm, target_ref),
                (weight_hbm.at[pl.ds(first, rows), :], sent),
            )
        )
    ]
    for copy in copies:
        copy.start()
    copies[3].wait()
    target = target_ref[...]
    owner = lax.shift_right_arithmetic(target, PIECE_BITS)
    place = jnp.where(target < 0, 0, (target & (PE - 1)) + 1).astype(F32)
    row, col = iota((slots, slots), 0), iota((slots, slots), 1)
    diagonal = row == col
    owner_col = jnp.sum(jnp.where(diagonal, owner, 0), axis=1, keepdims=True)
    place_col = jnp.sum(jnp.where(diagonal, place, 0.0), axis=1, keepdims=True)
    rank = jnp.sum(((owner_col == owner) & (row < col)).astype(jnp.int32), axis=0, keepdims=True)
    chosen = row // capacity
    if relative:
        chosen = chosen ^ lax.axis_index("seq")
    pick = ((chosen == owner) & (row % capacity == rank)).astype(F32).astype(BF16)
    marks = jnp.broadcast_to(place_col, (slots, LANES)).astype(BF16)

    copies[0].wait()
    x = x_ref[...]
    frames = [None] * FP
    bins = NFFT // 2
    later = iota((1, bins), 1) > 0
    for phase in range(4):
        shift = phase * (HOP % LANES)
        moved = x if phase == 0 else pltpu.roll(x, x.shape[1] - shift, 1)
        high = moved.astype(BF16)
        low = (moved - high.astype(F32)).astype(BF16)
        members = list(range(phase, FP, 4))
        starts = [HOP * f - shift for f in members]
        high = jnp.concatenate([high[:, s : s + NFFT] for s in starts], axis=0)
        low = jnp.concatenate([low[:, s : s + NFFT] for s in starts], axis=0)
        if phase == 0:
            copies[1].wait()
        table_high, table_low = fourier_ref[0], fourier_ref[1]
        spectra = dot(
            jnp.concatenate([high, low, high], axis=1),
            jnp.concatenate([table_high, table_high, table_low], axis=0),
        )
        squares = spectra * spectra
        if phase == 0:
            copies[2].wait()
        if phase == 0:
            filters = mel_ref[:bins, :]
            last_row = mel_ref[bins:, :].astype(F32)
            last_row = last_row[:1, :MEL] + last_row[:1, MEL:]
        last = squares[:, bins : bins + 1] * last_row
        power = squares[:, :bins] + jnp.where(later, squares[:, bins:], 0.0)
        power_high = power.astype(BF16)
        power_low = (power - power_high.astype(F32)).astype(BF16)
        both = dot(
            jnp.concatenate([power_high, power_low], axis=1),
            jnp.concatenate([filters, filters], axis=0),
        )
        energy = both[:, :MEL] + both[:, MEL:] + last
        log_mel = jnp.log(1.0 + energy).astype(BF16)
        for k, f in enumerate(members):
            frames[f] = log_mel[k * slots : (k + 1) * slots]
    packed = dot(pick, jnp.concatenate(frames + [marks], axis=1)).astype(BF16)
    count = slots // len(outs)
    for d, out in enumerate(outs):
        out[...] = packed[d * count : (d + 1) * count]
    copies[4].wait()


def place_kernel(*refs):
    parts, out = refs[:-1], refs[-1]
    rows = jnp.concatenate([part[...] for part in parts], axis=0)
    slots = rows.shape[0]
    mark = rows[:, MEL_WIDTH : MEL_WIDTH + LANES].astype(F32)[:, :1]
    row, col = iota((slots, slots), 0), iota((slots, slots), 1)
    mark = jnp.sum(jnp.where(row == col, mark, 0.0), axis=0, keepdims=True)
    at = iota((PE, slots), 0)
    groups = PE // GROUP
    wanted = (at % groups) * GROUP + at // groups + 1
    pick = (wanted.astype(F32) == mark).astype(F32).astype(BF16)
    out[...] = dot(pick, rows[:, :MEL_WIDTH]).astype(BF16)


def token_rows(pieces):
    groups = PE // GROUP
    pieces = pieces.astype(F32)
    rows = []
    for i in range(FP):
        cells = []
        for j in range(STACK):
            q, f = divmod(STACK * i + j, FP)
            cells.append(pieces[q * groups : (q + 1) * groups, f * MEL : (f + 1) * MEL])
        rows.append(jnp.concatenate(cells, axis=1))
    rows.append(jnp.zeros((ROWS - CH, STACK * MEL), F32))
    mixed = jnp.concatenate(rows, axis=0).astype(BF16)
    row, col = iota((ROWS, ROWS), 0), iota((ROWS, ROWS), 1)
    token = (col % groups) * FP + col // groups
    order = ((row == token) & (col < CH)).astype(F32).astype(BF16)
    return dot(order, mixed).astype(BF16)


def prepare_kernel(
    lengths_hbm, table_hbm, qkv_hbm, out_ref, qkv_ref, lengths_ref, table_ref, flipped, sems
):
    copies = [
        pltpu.make_async_copy(lengths_hbm, lengths_ref, sems.at[0]),
        pltpu.make_async_copy(table_hbm, table_ref, sems.at[1]),
        pltpu.make_async_copy(qkv_hbm, qkv_ref, sems.at[2]),
    ]
    for copy in copies:
        copy.start()
    copies[0].wait()
    copies[1].wait()
    pairs, blocks = out_ref.shape[:2]
    half = blocks * CH
    first = (lax.axis_index("seq") * lax.axis_size("sub") + lax.axis_index("sub")) * half
    total = lax.axis_size("seq") * lax.axis_size("sub") * half
    lane, row = iota((1, 3 * ROWS), 1), iota((ROWS, 1), 0)
    key_block = lane // ROWS
    key_place = lane - key_block * ROWS
    masks = []
    for c in range(blocks):
        query = first + c * CH + row
        key = first + (c - 1) * CH + key_block * CH + key_place
        query_utt, key_utt = jnp.zeros_like(query), jnp.zeros_like(key)
        end = jnp.int32(0)
        for r in range(lengths_ref.shape[0]):
            end = end + lengths_ref[r]
            query_utt = query_utt + (query >= end).astype(jnp.int32)
            key_utt = key_utt + (key >= end).astype(jnp.int32)
        inside = (key >= 0) & (key < total) & (key_place < CH)
        key_utt = jnp.where(inside, key_utt, -1)
        masks.append(jnp.where(query_utt == key_utt, 0.0, MASKED))
    heads, entries = table_ref.shape
    width = flipped.shape[1]
    mirror = iota((entries, width), 0) + iota((entries, width), 1) == entries - 1
    mirror = mirror.astype(F32).astype(BF16)
    rest, lines = table_ref[...], 0.0
    for _ in range(3):
        part = rest.astype(BF16)
        rest = rest - part.astype(F32)
        lines = lines + dot(part, mirror)
    flipped[...] = lines

    def one_head(head, side):
        line = jnp.broadcast_to(flipped[pl.ds(head, 1), :], (ROWS, width))
        turned = [
            pltpu.roll(line, (8 * b - (CH - 1)) % width, 1, stride=1, stride_axis=0)[:, : 3 * ROWS]
            for b in range(3)
        ]
        bias = jnp.where(
            key_block == 0, turned[0], jnp.where(key_block == 1, turned[1], turned[2])
        )
        for c in range(blocks):
            out_ref[head // 2, c, side * ROWS : (side + 1) * ROWS, :] = bias + masks[c]

    @pl.loop(0, pairs)
    def _(pair):
        one_head(2 * pair, 0)
        one_head(2 * pair + 1, 1)

    copies[2].wait()


def normalize(tokens, conv, conv_bias, gain, out):
    summed = dot(tokens, conv[...]) + conv_bias[...]
    features = (summed / (1.0 + jnp.exp(-summed))).astype(BF16).astype(F32)
    scale = 1.0 / features.shape[1]
    centred = features - jnp.sum(features, axis=1, keepdims=True) * scale
    variance = jnp.sum(centred * centred, axis=1, keepdims=True) * scale
    out[...] = (centred * lax.rsqrt(variance + EPSILON) * gain[...]).astype(BF16)


def own_kernel(n, *refs):
    pieces, parts, refs = refs[0], refs[1 : 2 * n], refs[2 * n :]
    bias_parts, gain_rows, refs = refs[:n], refs[n], refs[n + 1 :]
    qkv, q_out, k_out, v_out, conv, conv_bias, gain, normed = refs
    me, core = lax.axis_index("head"), lax.axis_index("sub")
    depth = parts[0].shape[1]
    for d in range(n):
        start = pl.multiple_of(lax.rem(me + d, n) * depth, depth)
        at = pl.ds(start, depth)
        lines = bias_parts[d][...].astype(F32)
        for k in range(depth // LANES):
            conv_bias[:, pl.ds(start + k * LANES, LANES)] = lines[k : k + 1]
        if d == 0:
            conv[:, at] = parts[0][...]
        else:
            got, swapped = parts[2 * d - 1 : 2 * d + 1]
            rows = got.shape[0]
            conv[pl.ds(pl.multiple_of(core * rows, rows), rows), at] = got[...]
            conv[pl.ds(pl.multiple_of((1 - core) * rows, rows), rows), at] = swapped[...]
    for k in range(gain_rows.shape[0]):
        gain[:, k * LANES : (k + 1) * LANES] = gain_rows[k : k + 1, :]
    normalize(token_rows(pieces[...]), conv, conv_bias, gain, normed)
    for p, out in enumerate((q_out, k_out, v_out)):
        out[0] = dot(normed[...], qkv[p]).astype(BF16)


def others_kernel(*refs):
    pieces = refs[:-8]
    conv, conv_bias, gain, qkv, *outs, normed = refs[-8:]
    tokens = jnp.concatenate([token_rows(piece[...]) for piece in pieces], axis=0)
    normalize(tokens, conv, conv_bias, gain, normed)
    for p, out in enumerate(outs):
        got = dot(normed[...], qkv[p]).astype(BF16)
        for k in range(len(pieces)):
            out[k] = got[k * ROWS : (k + 1) * ROWS]


def attend(q, k, v, bias):
    low_lanes = iota((ROWS, LANES), 1) < HDIM
    q = q * jnp.asarray(1.0 / math.sqrt(HDIM), BF16)
    zero = jnp.zeros_like(q)
    q = jnp.concatenate([jnp.where(low_lanes, q, zero), jnp.where(low_lanes, zero, q)], axis=0)
    scores = lax.dot_general(q, k, (((1,), (1,)), ((), ())), preferred_element_type=F32) + bias
    weights = jnp.exp(scores - jnp.max(scores, axis=1, keepdims=True))
    total = jnp.sum(weights, axis=1, keepdims=True)
    context = dot(weights.astype(BF16), v) * (1.0 / total)
    return jnp.where(low_lanes, context[:ROWS], context[ROWS:])


def inner_kernel(n, *refs):
    own, others, near = refs[:3], refs[3:6], refs[6]
    conv, conv_bias, gain, qkv, bias, out, keys, values, queries, normed = refs[7:]
    me, core = lax.axis_index("head"), lax.axis_index("sub")
    for source, target, first in zip(own, (queries, keys, values), (0, 1, 1)):
        target[first + me] = source[0]
    for d in range(1, n):
        for source, target, first in zip(others, (queries, keys, values), (0, 1, 1)):
            target[first + lax.rem(me + d, n)] = source[d - 1]
    normalize(token_rows(near[...]), conv, conv_bias, gain, normed)
    place = jnp.where(core == 0, n + 1, 0)
    keys[place] = dot(normed[...], qkv[1]).astype(BF16)
    values[place] = dot(normed[...], qkv[2]).astype(BF16)
    for k in range(n - 1):
        c = k + 1 - core
        for pair in range(qkv.shape[2] // LANES):
            at = slice(pair * LANES, (pair + 1) * LANES)
            out[k, :, at] = attend(
                queries[c, :, at],
                keys[pl.ds(c, 3), :, at].reshape(3 * ROWS, LANES),
                values[pl.ds(c, 3), :, at].reshape(3 * ROWS, LANES),
                bias[pair, c],
            ).astype(BF16)
    edge = jnp.where(core == 0, 0, n - 1)
    queries[0] = queries[edge]
    first = jnp.where(core == 0, 1, n - 1)
    for target in (keys, values):
        kept = target[pl.ds(first, 2)]
        target[0] = kept[0]
        target[1] = kept[1]


def outer_kernel(n, *refs):
    inner, keys, values, queries, far, conv, conv_bias, gain, qkv, bias = refs[:10]
    out, all_keys, all_values, normed = refs[10:]
    core = lax.axis_index("sub")
    normalize(token_rows(far[...]), conv, conv_bias, gain, normed)
    for p, source, target in ((1, keys, all_keys), (2, values, all_values)):
        target[1 - core] = source[0]
        target[2 - core] = source[1]
        target[2 * core] = dot(normed[...], qkv[p]).astype(BF16)
    c = jnp.where(core == 0, 0, n - 1)
    for pair in range(qkv.shape[2] // LANES):
        at = slice(pair * LANES, (pair + 1) * LANES)
        context = attend(
            queries[0, :, at],
            all_keys[:, :, at].reshape(3 * ROWS, LANES),
            all_values[:, :, at].reshape(3 * ROWS, LANES),
            bias[pair, c],
        ).astype(BF16)
        context = context.astype(F32)[:CH]
        done = [inner[k, :, at].astype(F32)[:CH] for k in range(n - 1)]
        out[:, at] = jnp.where(
            core == 0,
            jnp.concatenate([context] + done, axis=0),
            jnp.concatenate(done + [context], axis=0),
        ).astype(BF16)


def vmem(count):
    return [pl.BlockSpec(memory_space=pltpu.VMEM)] * count


def from_hbm(array):
    return pltpu.with_memory_space_constraint(array, pltpu.HBM)


def in_vmem(array):
    return pltpu.with_memory_space_constraint(array, pltpu.VMEM)


def from_heads(block, n):
    return [lax.ppermute(block, "head", [((i + d) % n, i) for i in range(n)]) for d in range(1, n)]


def local(
    wave_pieces, piece_target, utt_lengths, sub_weight, sub_bias, norm_gain, qkv_weight, rel_bias
):
    shards, n, cores = lax.axis_size("seq"), lax.axis_size("head"), lax.axis_size("sub")
    assert cores == 2
    slots, length = wave_pieces.shape[3:]
    capacity = slots // shards
    relative = shards in (2, 4) and capacity % 16 == 0
    outs = shards if relative else 1
    payload = MEL_WIDTH + LANES
    fourier, filters = fourier_tables(), mel_tables()
    in_hbm = pl.BlockSpec(memory_space=pltpu.HBM)
    conv_rows = sub_weight.shape[0]
    bias_got = from_heads(sub_bias, n)
    weight_sent, *packed = pl.pallas_call(
        functools.partial(mel_kernel, shards, capacity, relative),
        out_shape=[jax.ShapeDtypeStruct((conv_rows // cores, sub_weight.shape[1]), BF16)]
        + [jax.ShapeDtypeStruct((slots // outs, payload), BF16)] * outs,
        in_specs=[in_hbm] * 5,
        out_specs=vmem(outs + 1),
        scratch_shapes=[
            pltpu.VMEM((slots, length), F32),
            pltpu.VMEM((1, slots), jnp.int32),
            pltpu.VMEM(fourier.shape, BF16),
            pltpu.VMEM(filters.shape, BF16),
            pltpu.SemaphoreType.DMA((5,)),
        ],
        compiler_params=pltpu.CompilerParams(vmem_limit_bytes=24 << 20),
        name="log_mel",
    )(
        from_hbm(wave_pieces.reshape(slots, length)),
        from_hbm(piece_target.reshape(1, slots)),
        from_hbm(sub_weight),
        from_hbm(jnp.asarray(fourier)),
        from_hbm(jnp.asarray(filters)),
    )
    if relative:
        received = [packed[0]] + [
            lax.ppermute(packed[d], "seq", [(i, i ^ d) for i in range(shards)])
            for d in range(1, shards)
        ]
    else:
        blocks = packed[0].reshape(shards, capacity, payload)
        blocks = lax.all_to_all(blocks, "seq", split_axis=0, concat_axis=0, tiled=True)
        received = [blocks.reshape(slots, payload)]

    weight_got = from_heads(weight_sent, n)

    local_width = qkv_weight.shape[2]
    pairs = local_width // LANES
    gain = norm_gain.reshape(-1, LANES)
    me, core = lax.axis_index("head"), lax.axis_index("sub")
    last, first = lax.rem(n - 1 - me + n, n), lax.rem(n - me, n)
    near_at, far_at = jnp.where(core == 0, last, first), jnp.where(core == 0, first, last)
    near_is, far_is = [near_at == d for d in range(n)], [far_at == d for d in range(n)]
    conv_bias = [part.reshape(-1, LANES) for part in [sub_bias] + bias_got]
    rel_bias, gain, near_is, far_is, _ = lax.optimization_barrier(
        (rel_bias, gain, near_is, far_is, packed[0])
    )
    entries = rel_bias.shape[1]
    qkv = jnp.transpose(qkv_weight, (1, 0, 2))
    bias, qkv = pl.pallas_call(
        prepare_kernel,
        out_shape=[
            pltpu.VMEM((pairs, n, 2 * ROWS, 3 * ROWS), F32),
            pltpu.VMEM(qkv.shape, BF16),
        ],
        in_specs=[in_hbm] * 3,
        out_specs=vmem(2),
        scratch_shapes=[
            pltpu.SMEM(utt_lengths.shape, jnp.int32),
            pltpu.VMEM(rel_bias.shape, F32),
            pltpu.VMEM((2 * pairs, entries + -entries % LANES), F32),
            pltpu.SemaphoreType.DMA((3,)),
        ],
        compiler_params=pltpu.CompilerParams(vmem_limit_bytes=8 << 20),
        cost_estimate=pl.CostEstimate(flops=1 << 31, bytes_accessed=8 << 20, transcendentals=0),
        name="prepare",
    )(from_hbm(utt_lengths), from_hbm(rel_bias), from_hbm(qkv))
    received, weight_got, conv_bias, bias, qkv, gain, near_is, far_is = lax.optimization_barrier(
        (received, weight_got, conv_bias, bias, qkv, gain, near_is, far_is)
    )
    conv = [sub_weight]
    for got in weight_got:
        conv += [got, lax.ppermute(got, "sub", [(0, 1), (1, 0)])]

    own = pl.pallas_call(
        place_kernel,
        out_shape=jax.ShapeDtypeStruct((PE, MEL_WIDTH), BF16),
        in_specs=vmem(len(received)),
        out_specs=vmem(1)[0],
        compiler_params=pltpu.CompilerParams(vmem_limit_bytes=8 << 20),
        name="place",
    )(*received)

    others = from_heads(own, n)
    near_sent = far_sent = own
    for d in range(1, n):
        near_sent = jnp.where(near_is[d], others[d - 1], near_sent)
        far_sent = jnp.where(far_is[d], others[d - 1], far_sent)
    near = lax.ppermute(near_sent, "sub", [(0, 1), (1, 0)])
    swaps = [(cores * k + 1, cores * k + 2) for k in range(shards - 1)]
    far = lax.ppermute(far_sent, ("seq", "sub"), swaps + [(b, a) for a, b in swaps])

    width = qkv_weight.shape[0]
    qkv = in_vmem(qkv)
    limit = pltpu.CompilerParams(vmem_limit_bytes=16 << 20)
    *own_qkv, whole, whole_bias, whole_gain = pl.pallas_call(
        functools.partial(own_kernel, n),
        out_shape=[jax.ShapeDtypeStruct((1, ROWS, local_width), BF16)] * 3
        + [
            jax.ShapeDtypeStruct((sub_weight.shape[0], width), BF16),
            jax.ShapeDtypeStruct((1, width), F32),
            jax.ShapeDtypeStruct((1, width), F32),
        ],
        in_specs=vmem(1 + len(conv) + n + 2),
        out_specs=vmem(6),
        scratch_shapes=[pltpu.VMEM((ROWS, width), BF16)],
        compiler_params=limit,
        cost_estimate=pl.CostEstimate(flops=2 << 30, bytes_accessed=9 << 20, transcendentals=0),
        name="own",
    )(own, *conv, *conv_bias, gain, qkv)
    weights = (whole, whole_bias, whole_gain, qkv)
    other_qkv = pl.pallas_call(
        others_kernel,
        out_shape=[jax.ShapeDtypeStruct((n - 1, ROWS, local_width), BF16)] * 3,
        in_specs=vmem(n - 1 + len(weights)),
        out_specs=vmem(3),
        scratch_shapes=[pltpu.VMEM(((n - 1) * ROWS, width), BF16)],
        compiler_params=limit,
        cost_estimate=pl.CostEstimate(flops=2 << 30, bytes_accessed=9 << 20, transcendentals=0),
        name="others",
    )(*others, *weights)
    inner, keys, values, queries = pl.pallas_call(
        functools.partial(inner_kernel, n),
        out_shape=[
            jax.ShapeDtypeStruct((n - 1, ROWS, local_width), BF16),
            jax.ShapeDtypeStruct((n + 2, ROWS, local_width), BF16),
            jax.ShapeDtypeStruct((n + 2, ROWS, local_width), BF16),
            jax.ShapeDtypeStruct((n, ROWS, local_width), BF16),
        ],
        in_specs=vmem(7 + len(weights) + 1),
        out_specs=vmem(4),
        scratch_shapes=[pltpu.VMEM((ROWS, width), BF16)],
        compiler_params=limit,
        cost_estimate=pl.CostEstimate(flops=4 << 30, bytes_accessed=9 << 20, transcendentals=0),
        name="inner",
    )(*own_qkv, *other_qkv, near, *weights, in_vmem(bias))
    return pl.pallas_call(
        functools.partial(outer_kernel, n),
        out_shape=jax.ShapeDtypeStruct((n * CH, local_width), BF16),
        in_specs=vmem(5 + len(weights) + 1),
        out_specs=vmem(1)[0],
        scratch_shapes=[
            pltpu.VMEM((3, ROWS, local_width), BF16),
            pltpu.VMEM((3, ROWS, local_width), BF16),
            pltpu.VMEM((ROWS, width), BF16),
        ],
        compiler_params=limit,
        name="outer",
    )(inner, keys, values, queries, far, *weights, in_vmem(bias))


def solution(mesh):
    placed = (
        P(("groups", "seq"), "head", "sub", None, None),
        P(("groups", "seq"), "head", "sub", None),
        P("groups"),
        P(None, "head"),
        P("head"),
        P(),
        P(None, None, "head"),
        P("head", None),
    )
    return jax.shard_map(
        local,
        mesh=mesh,
        in_specs=placed,
        out_specs=P(("groups", "seq", "sub"), "head"),
        check_vma=False,
    )
```

```python
import functools
import math

import jax
import jax.numpy as jnp
import ml_dtypes
import numpy as np
from jax import lax
from jax.experimental import pallas as pl
from jax.experimental.pallas import tpu as pltpu
from jax.sharding import PartitionSpec as P

HDIM = 64
MEL = 128
NFFT = 512
HOP = 160
FP = 17
CH = 136
PE = 32

SAMPLE_RATE = 16000.0
EPSILON = 1e-05
MASKED = -1e30

LANES = 128
PIECE_BITS = 5
ROWS = 144
GROUP = 4
STACK = 4
MEL_WIDTH = FP * MEL
BF16 = jnp.bfloat16
F32 = jnp.float32


def split_bf16(values):
    high = values.astype(ml_dtypes.bfloat16)
    low = (values - high.astype(np.float64)).astype(ml_dtypes.bfloat16)
    return np.stack([high, low])


def fourier_tables():
    n, bins = np.arange(NFFT // 2)[:, None], NFFT // 2

    def phase(k):
        return 2.0 * np.pi * ((n * k[None, :]) % NFFT) / NFFT

    even, odd = np.arange(0, bins, 2), np.arange(1, bins, 2)
    sine = np.sin(phase(even))
    sine[:, 0] = np.cos(phase(np.array([bins])))[:, 0]
    return np.stack(
        [
            split_bf16(np.concatenate([np.cos(phase(even)), sine], axis=1)),
            split_bf16(np.concatenate([np.cos(phase(odd)), np.sin(phase(odd))], axis=1)),
        ]
    )


def window_halves():
    window = 0.5 - 0.5 * np.cos(2.0 * np.pi * np.arange(NFFT) / NFFT)
    return window.reshape(2, NFFT // 2).astype(np.float32)


def mel_tables():
    bins = NFFT // 2
    highest = 2595.0 * math.log10(1.0 + SAMPLE_RATE / 2.0 / 700.0)
    points = np.arange(MEL + 2) * (highest / (MEL + 1))
    hertz = 700.0 * (10.0 ** (points / 2595.0) - 1.0)
    centres = np.arange(bins + 1) * (SAMPLE_RATE / NFFT)
    rising = (centres[:, None] - hertz[None, :-2]) / (hertz[1:-1] - hertz[:-2])[None, :]
    falling = (hertz[None, 2:] - centres[:, None]) / (hertz[2:] - hertz[1:-1])[None, :]
    filters = np.maximum(0.0, np.minimum(rising, falling))
    filters = [filters[0:bins:2], filters[1:bins:2], filters[bins:], np.zeros((15, MEL))]
    high, low = split_bf16(np.concatenate(filters, axis=0))
    return np.concatenate([high, low], axis=1)


def dot(a, b):
    return jnp.dot(a, b, preferred_element_type=F32)


def iota(shape, dim):
    return lax.broadcasted_iota(jnp.int32, shape, dim)


def mel_kernel(shards, capacity, relative, *refs):
    sources, outs = refs[:5], refs[5:-6]
    targets, sems = refs[-6:-1], refs[-1]
    x_ref, target_ref, window_ref, fourier_ref, mel_ref = targets
    slots = x_ref.shape[0]
    pairs = zip(sources, targets)
    copies = [pltpu.make_async_copy(*pair, sems.at[k]) for k, pair in enumerate(pairs)]
    for copy in copies:
        copy.start()
    copies[1].wait()
    target = target_ref[...]
    owner = lax.shift_right_arithmetic(target, PIECE_BITS)
    place = jnp.where(target < 0, 0, (target & (PE - 1)) + 1).astype(F32)
    row, col = iota((slots, slots), 0), iota((slots, slots), 1)
    diagonal = row == col
    owner_col = jnp.sum(jnp.where(diagonal, owner, 0), axis=1, keepdims=True)
    place_col = jnp.sum(jnp.where(diagonal, place, 0.0), axis=1, keepdims=True)
    rank = jnp.sum(((owner_col == owner) & (row < col)).astype(jnp.int32), axis=0, keepdims=True)
    chosen = row // capacity
    if relative:
        chosen = chosen ^ lax.axis_index("seq")
    pick = ((chosen == owner) & (row % capacity == rank)).astype(F32).astype(BF16)
    marks = jnp.broadcast_to(place_col, (slots, LANES)).astype(BF16)

    copies[0].wait()
    copies[2].wait()
    x = x_ref[...]
    frames = [None] * FP
    half, bins = NFFT // 2, NFFT // 4
    rising, falling = window_ref[0:1, :], window_ref[1:2, :]
    later = iota((1, bins), 1) > 0
    for phase in range(4):
        shift = phase * (HOP % LANES)
        moved = x if phase == 0 else pltpu.roll(x, x.shape[1] - shift, 1)
        members = list(range(phase, FP, 4))
        sums, differences = [], []
        for f in members:
            start = HOP * f - shift
            left = moved[:, start : start + half] * rising
            right = moved[:, start + half : start + NFFT] * falling
            sums.append(left + right)
            differences.append(left - right)
        squares = []
        for k, parts in enumerate((sums, differences)):
            values = jnp.concatenate(parts, axis=0)
            high = values.astype(BF16)
            low = (values - high.astype(F32)).astype(BF16)
            if phase == 0 and k == 0:
                copies[3].wait()
            table_high, table_low = fourier_ref[k, 0], fourier_ref[k, 1]
            spectra = dot(
                jnp.concatenate([high, low, high], axis=1),
                jnp.concatenate([table_high, table_high, table_low], axis=0),
            )
            squares.append(spectra * spectra)
        if phase == 0:
            copies[4].wait()
            filters = mel_ref[:half, :]
            last_row = mel_ref[half:, :].astype(F32)
            last_row = last_row[:1, :MEL] + last_row[:1, MEL:]
        even, odd = squares
        last = even[:, bins : bins + 1] * last_row
        even = even[:, :bins] + jnp.where(later, even[:, bins:], 0.0)
        power = jnp.concatenate([even, odd[:, :bins] + odd[:, bins:]], axis=1)
        power_high = power.astype(BF16)
        power_low = (power - power_high.astype(F32)).astype(BF16)
        both = dot(
            jnp.concatenate([power_high, power_low], axis=1),
            jnp.concatenate([filters, filters], axis=0),
        )
        energy = both[:, :MEL] + both[:, MEL:] + last
        log_mel = jnp.log(1.0 + energy).astype(BF16)
        for k, f in enumerate(members):
            frames[f] = log_mel[k * slots : (k + 1) * slots]
    packed = dot(pick, jnp.concatenate(frames + [marks], axis=1)).astype(BF16)
    count = slots // len(outs)
    for d, out in enumerate(outs):
        out[...] = packed[d * count : (d + 1) * count]


def place_kernel(*refs):
    parts, out = refs[:-1], refs[-1]
    rows = jnp.concatenate([part[...] for part in parts], axis=0)
    slots = rows.shape[0]
    mark = rows[:, MEL_WIDTH : MEL_WIDTH + LANES].astype(F32)[:, :1]
    row, col = iota((slots, slots), 0), iota((slots, slots), 1)
    mark = jnp.sum(jnp.where(row == col, mark, 0.0), axis=0, keepdims=True)
    at = iota((PE, slots), 0)
    groups = PE // GROUP
    wanted = (at % groups) * GROUP + at // groups + 1
    pick = (wanted.astype(F32) == mark).astype(F32).astype(BF16)
    out[...] = dot(pick, rows[:, :MEL_WIDTH]).astype(BF16)


def token_rows(pieces):
    groups = PE // GROUP
    pieces = pieces.astype(F32)
    rows = []
    for i in range(FP):
        cells = []
        for j in range(STACK):
            q, f = divmod(STACK * i + j, FP)
            cells.append(pieces[q * groups : (q + 1) * groups, f * MEL : (f + 1) * MEL])
        rows.append(jnp.concatenate(cells, axis=1))
    rows.append(jnp.zeros((ROWS - CH, STACK * MEL), F32))
    mixed = jnp.concatenate(rows, axis=0).astype(BF16)
    row, col = iota((ROWS, ROWS), 0), iota((ROWS, ROWS), 1)
    token = (col % groups) * FP + col // groups
    order = ((row == token) & (col < CH)).astype(F32).astype(BF16)
    return dot(order, mixed).astype(BF16)


def prepare_kernel(
    lengths_hbm, table_hbm, qkv_hbm, out_ref, qkv_ref, lengths_ref, table_ref, flipped, sems
):
    copies = [
        pltpu.make_async_copy(lengths_hbm, lengths_ref, sems.at[0]),
        pltpu.make_async_copy(table_hbm, table_ref, sems.at[1]),
        pltpu.make_async_copy(qkv_hbm, qkv_ref, sems.at[2]),
    ]
    for copy in copies:
        copy.start()
    copies[0].wait()
    copies[1].wait()
    pairs, blocks = out_ref.shape[:2]
    half = blocks * CH
    first = (lax.axis_index("seq") * lax.axis_size("sub") + lax.axis_index("sub")) * half
    total = lax.axis_size("seq") * lax.axis_size("sub") * half
    lane, row = iota((1, 3 * ROWS), 1), iota((ROWS, 1), 0)
    orders = ((0, 1, 2), (2, 0, 1))
    slot = lane // ROWS
    key_place = lane - slot * ROWS
    masks = []
    for c in range(blocks):
        order = orders[1 if c == blocks - 1 else 0]
        key_block = jnp.where(slot == 0, order[0], jnp.where(slot == 1, order[1], order[2]))
        query = first + c * CH + row
        key = first + (c - 1) * CH + key_block * CH + key_place
        query_utt, key_utt = jnp.zeros_like(query), jnp.zeros_like(key)
        end = jnp.int32(0)
        for r in range(lengths_ref.shape[0]):
            end = end + lengths_ref[r]
            query_utt = query_utt + (query >= end).astype(jnp.int32)
            key_utt = key_utt + (key >= end).astype(jnp.int32)
        inside = (key >= 0) & (key < total) & (key_place < CH)
        key_utt = jnp.where(inside, key_utt, -1)
        masks.append(jnp.where(query_utt == key_utt, 0.0, MASKED))
    heads, entries = table_ref.shape
    width = flipped.shape[1]
    mirror = iota((entries, width), 0) + iota((entries, width), 1) == entries - 1
    mirror = mirror.astype(F32).astype(BF16)
    rest, lines = table_ref[...], 0.0
    for _ in range(3):
        part = rest.astype(BF16)
        rest = rest - part.astype(F32)
        lines = lines + dot(part, mirror)
    flipped[...] = lines

    def one_head(head, side):
        line = jnp.broadcast_to(flipped[pl.ds(head, 1), :], (ROWS, width))
        biases = []
        for order in orders:
            turned = [
                pltpu.roll(
                    line, (ROWS * at - CH * b - (CH - 1)) % width, 1, stride=1, stride_axis=0
                )[:, : 3 * ROWS]
                for at, b in enumerate(order)
            ]
            biases.append(
                jnp.where(slot == 0, turned[0], jnp.where(slot == 1, turned[1], turned[2]))
            )
        for c in range(blocks):
            bias = biases[1 if c == blocks - 1 else 0]
            out_ref[head // 2, c, side * ROWS : (side + 1) * ROWS, :] = bias + masks[c]

    @pl.loop(0, pairs)
    def _(pair):
        one_head(2 * pair, 0)
        one_head(2 * pair + 1, 1)

    copies[2].wait()


def normalize(tokens, conv, conv_bias, gain, out):
    summed = dot(tokens, conv[...]) + conv_bias[...]
    features = (summed / (1.0 + jnp.exp(-summed))).astype(BF16).astype(F32)
    scale = 1.0 / features.shape[1]
    centred = features - jnp.sum(features, axis=1, keepdims=True) * scale
    variance = jnp.sum(centred * centred, axis=1, keepdims=True) * scale
    out[...] = (centred * lax.rsqrt(variance + EPSILON) * gain[...]).astype(BF16)


def half_kernel(n, *refs):
    pieces, parts, bias_parts = refs[:n], refs[n : 3 * n - 1], refs[3 * n - 1 : 4 * n - 1]
    gain_rows, qkv, *outs, sent, conv, conv_bias, gain, normed = refs[4 * n - 1 :]
    me, core = lax.axis_index("head"), lax.axis_index("sub")
    depth = parts[0].shape[1]
    for d in range(n):
        start = pl.multiple_of(lax.rem(me + d, n) * depth, depth)
        at = pl.ds(start, depth)
        lines = bias_parts[d][...].astype(F32)
        for k in range(depth // LANES):
            conv_bias[:, pl.ds(start + k * LANES, LANES)] = lines[k : k + 1]
        if d == 0:
            conv[:, at] = parts[0][...]
        else:
            got, passed = parts[2 * d - 1 : 2 * d + 1]

            @pl.when(core == 0)
            def _(got=got, at=at):
                conv[:, at] = got[...]

            @pl.when(core == 1)
            def _(passed=passed, at=at):
                conv[:, at] = passed[...]

    for k in range(gain_rows.shape[0]):
        gain[:, k * LANES : (k + 1) * LANES] = gain_rows[k : k + 1, :]
    tokens = jnp.concatenate([token_rows(piece[...]) for piece in pieces], axis=0)
    normalize(tokens, conv, conv_bias, gain, normed)
    wanted = jnp.where(core == 0, n - 1, 0)
    for p, out in enumerate(outs):
        got = dot(normed[...], qkv[p]).astype(BF16)
        for d in range(n):
            out[lax.rem(me + d, n)] = got[d * ROWS : (d + 1) * ROWS]
        if p > 0:
            sent[p - 1] = out[wanted]


def attend(q, k, v, bias):
    low_lanes = iota((ROWS, LANES), 1) < HDIM
    q = q * jnp.asarray(1.0 / math.sqrt(HDIM), BF16)
    zero = jnp.zeros_like(q)
    q = jnp.concatenate([jnp.where(low_lanes, q, zero), jnp.where(low_lanes, zero, q)], axis=0)
    scores = lax.dot_general(q, k, (((1,), (1,)), ((), ())), preferred_element_type=F32) + bias
    weights = jnp.exp(scores - jnp.max(scores, axis=1, keepdims=True)).astype(BF16)
    summed = dot(weights, jnp.concatenate([v, jnp.ones_like(v)], axis=1))
    context = summed[:, :LANES] * (1.0 / summed[:, LANES:])
    return jnp.where(low_lanes, context[:ROWS], context[ROWS:])


def edge_context(pair, block, halo_keys, halo_values, first, queries, keys, values, bias):
    at = slice(pair * LANES, (pair + 1) * LANES)
    return attend(
        queries[block, :, at],
        jnp.concatenate([halo_keys[:, at], keys[first, :, at], keys[first + 1, :, at]], axis=0),
        jnp.concatenate(
            [halo_values[:, at], values[first, :, at], values[first + 1, :, at]], axis=0
        ),
        bias[pair, block],
    )


def far_kernel(n, *refs):
    queries, keys, values, far, conv, conv_bias, gain, qkv, bias, out = refs[:10]
    normed, far_keys, far_values = refs[10:]
    core = lax.axis_index("sub")
    normalize(token_rows(far[...]), conv, conv_bias, gain, normed)
    far_keys[...] = dot(normed[...], qkv[1]).astype(BF16)
    far_values[...] = dot(normed[...], qkv[2]).astype(BF16)
    block, first = jnp.where(core == 0, 0, n - 1), jnp.where(core == 0, 0, n - 2)
    for pair in range(qkv.shape[2] // LANES):
        context = edge_context(
            pair, block, far_keys, far_values, first, queries, keys, values, bias
        )
        out[:, pair * LANES : (pair + 1) * LANES] = context.astype(BF16)


def near_kernel(n, *refs):
    queries, keys, values, near, far_context, bias, out = refs
    core = lax.axis_index("sub")
    block, first = jnp.where(core == 0, n - 1, 0), jnp.where(core == 0, n - 2, 0)
    for pair in range(queries.shape[2] // LANES):
        at = slice(pair * LANES, (pair + 1) * LANES)
        context = edge_context(
            pair, block, near.at[0], near.at[1], first, queries, keys, values, bias
        )[:CH]
        middle = [
            attend(
                queries[c, :, at],
                keys[c - 1 : c + 2, :, at].reshape(3 * ROWS, LANES),
                values[c - 1 : c + 2, :, at].reshape(3 * ROWS, LANES),
                bias[pair, c],
            )[:CH]
            for c in range(1, n - 1)
        ]
        other = far_context[:, at].astype(F32)[:CH]
        out[:, at] = jnp.where(
            core == 0,
            jnp.concatenate([other] + middle + [context], axis=0),
            jnp.concatenate([context] + middle + [other], axis=0),
        ).astype(BF16)


def vmem(count):
    return [pl.BlockSpec(memory_space=pltpu.VMEM)] * count


def from_hbm(array):
    return pltpu.with_memory_space_constraint(array, pltpu.HBM)


def in_vmem(array):
    return pltpu.with_memory_space_constraint(array, pltpu.VMEM)


def from_heads(block, n):
    return [lax.ppermute(block, "head", [((i + d) % n, i) for i in range(n)]) for d in range(1, n)]


def local(
    wave_pieces, piece_target, utt_lengths, sub_weight, sub_bias, norm_gain, qkv_weight, rel_bias
):
    shards, n, cores = lax.axis_size("seq"), lax.axis_size("head"), lax.axis_size("sub")
    assert cores == 2
    slots, length = wave_pieces.shape[3:]
    capacity = slots // shards
    relative = shards in (2, 4) and capacity % 16 == 0
    outs = shards if relative else 1
    payload = MEL_WIDTH + LANES
    fourier, filters, window = fourier_tables(), mel_tables(), window_halves()
    in_hbm = pl.BlockSpec(memory_space=pltpu.HBM)
    groups = lax.axis_size("groups")
    weight_got = []
    for d in range(1, n):
        links = []
        for g in range(groups):
            for h in range(n):
                at = (g * n + h) * cores
                links.append(((g * n + (h + d) % n) * cores, at))
                links.append((((g + 1) % groups * n + h) * cores + 1, at + 1))
        weight_got.append(lax.ppermute(sub_weight, ("groups", "head", "sub"), links))
    packed = pl.pallas_call(
        functools.partial(mel_kernel, shards, capacity, relative),
        out_shape=[jax.ShapeDtypeStruct((slots // outs, payload), BF16)] * outs,
        in_specs=[in_hbm] * 5,
        out_specs=vmem(outs),
        scratch_shapes=[
            pltpu.VMEM((slots, length), F32),
            pltpu.VMEM((1, slots), jnp.int32),
            pltpu.VMEM(window.shape, F32),
            pltpu.VMEM(fourier.shape, BF16),
            pltpu.VMEM(filters.shape, BF16),
            pltpu.SemaphoreType.DMA((5,)),
        ],
        compiler_params=pltpu.CompilerParams(vmem_limit_bytes=24 << 20),
        name="log_mel",
    )(
        from_hbm(wave_pieces.reshape(slots, length)),
        from_hbm(piece_target.reshape(1, slots)),
        from_hbm(jnp.asarray(window)),
        from_hbm(jnp.asarray(fourier)),
        from_hbm(jnp.asarray(filters)),
    )
    if relative:
        received = [
            lax.ppermute(packed[d], "seq", [(i, i ^ d) for i in range(shards)])
            for d in range(shards - 1, 0, -1)
        ] + [packed[0]]
    else:
        blocks = packed[0].reshape(shards, capacity, payload)
        blocks = lax.all_to_all(blocks, "seq", split_axis=0, concat_axis=0, tiled=True)
        received = [blocks.reshape(slots, payload)]

    local_width = qkv_weight.shape[2]
    pairs = local_width // LANES
    gain = norm_gain.reshape(-1, LANES)
    me, core = lax.axis_index("head"), lax.axis_index("sub")
    last, first = lax.rem(n - 1 - me + n, n), lax.rem(n - me, n)
    far_at = jnp.where(core == 0, first, last)
    far_is = [far_at == d for d in range(n)]
    rel_bias, gain, far_is, _ = lax.optimization_barrier(
        (rel_bias, gain, far_is, packed[0])
    )
    entries = rel_bias.shape[1]
    qkv = jnp.transpose(qkv_weight, (1, 0, 2))
    bias, qkv = pl.pallas_call(
        prepare_kernel,
        out_shape=[
            pltpu.VMEM((pairs, n, 2 * ROWS, 3 * ROWS), F32),
            pltpu.VMEM(qkv.shape, BF16),
        ],
        in_specs=[in_hbm] * 3,
        out_specs=vmem(2),
        scratch_shapes=[
            pltpu.SMEM(utt_lengths.shape, jnp.int32),
            pltpu.VMEM(rel_bias.shape, F32),
            pltpu.VMEM((2 * pairs, entries + -entries % LANES), F32),
            pltpu.SemaphoreType.DMA((3,)),
        ],
        compiler_params=pltpu.CompilerParams(vmem_limit_bytes=8 << 20),
        cost_estimate=pl.CostEstimate(flops=1 << 31, bytes_accessed=8 << 20, transcendentals=0),
        name="prepare",
    )(from_hbm(utt_lengths), from_hbm(rel_bias), from_hbm(qkv))
    received, weight_got, bias, qkv, gain, far_is = lax.optimization_barrier(
        (received, weight_got, bias, qkv, gain, far_is)
    )
    own = pl.pallas_call(
        place_kernel,
        out_shape=jax.ShapeDtypeStruct((PE, MEL_WIDTH), BF16),
        in_specs=vmem(len(received)),
        out_specs=vmem(1)[0],
        compiler_params=pltpu.CompilerParams(vmem_limit_bytes=8 << 20),
        name="place",
    )(*received)
    bias_sent, _ = lax.optimization_barrier((sub_bias, own))
    bias_lines = [part.reshape(-1, LANES) for part in [sub_bias] + from_heads(bias_sent, n)]
    conv = [sub_weight]
    for got in weight_got:
        got, _ = lax.optimization_barrier((got, own))
        conv += [got, lax.ppermute(got, "sub", [(0, 1), (1, 0)])]

    others = from_heads(own, n)
    width = qkv_weight.shape[0]
    qkv = in_vmem(qkv)
    limit = pltpu.CompilerParams(vmem_limit_bytes=16 << 20)
    far_sent = own
    for d in range(1, n):
        far_sent = jnp.where(far_is[d], others[d - 1], far_sent)
    links = []
    for h in range(n):
        for k in range(shards - 1):
            above, below = ((k + 1) * n + h) * cores, (k * n + h) * cores + 1
            links += [(above, below), (below, above)]
        links.append((h * cores, (h + 1) % n * cores))
        ends = (shards - 1) * n
        links.append(((ends + h) * cores + 1, (ends + (h + 1) % n) * cores + 1))
    far = lax.ppermute(far_sent, ("seq", "head", "sub"), links)
    *half_qkv, near_sent, whole, whole_bias, whole_gain = pl.pallas_call(
        functools.partial(half_kernel, n),
        out_shape=[jax.ShapeDtypeStruct((n, ROWS, local_width), BF16)] * 3
        + [
            jax.ShapeDtypeStruct((2, ROWS, local_width), BF16),
            jax.ShapeDtypeStruct((sub_weight.shape[0], width), BF16),
            jax.ShapeDtypeStruct((1, width), F32),
            jax.ShapeDtypeStruct((1, width), F32),
        ],
        in_specs=vmem(n + len(conv) + n + 2),
        out_specs=vmem(7),
        scratch_shapes=[pltpu.VMEM((n * ROWS, width), BF16)],
        compiler_params=limit,
        cost_estimate=pl.CostEstimate(flops=4 << 30, bytes_accessed=9 << 20, transcendentals=0),
        name="half",
    )(own, *others, *conv, *bias_lines, gain, qkv)
    weights = (whole, whole_bias, whole_gain, qkv)
    near = lax.ppermute(near_sent, "sub", [(0, 1), (1, 0)])
    far_context = pl.pallas_call(
        functools.partial(far_kernel, n),
        out_shape=jax.ShapeDtypeStruct((ROWS, local_width), BF16),
        in_specs=vmem(4 + len(weights) + 1),
        out_specs=vmem(1)[0],
        scratch_shapes=[
            pltpu.VMEM((ROWS, width), BF16),
            pltpu.VMEM((ROWS, local_width), BF16),
            pltpu.VMEM((ROWS, local_width), BF16),
        ],
        compiler_params=limit,
        cost_estimate=pl.CostEstimate(flops=16 << 30, bytes_accessed=9 << 20, transcendentals=0),
        name="far",
    )(*half_qkv, far, *weights, in_vmem(bias))
    return pl.pallas_call(
        functools.partial(near_kernel, n),
        out_shape=jax.ShapeDtypeStruct((n * CH, local_width), BF16),
        in_specs=vmem(6),
        out_specs=vmem(1)[0],
        compiler_params=limit,
        name="near",
    )(*half_qkv, near, far_context, in_vmem(bias))


def solution(mesh):
    placed = (
        P(("groups", "seq"), "head", "sub", None, None),
        P(("groups", "seq"), "head", "sub", None),
        P("groups"),
        P(None, "head"),
        P("head"),
        P(),
        P(None, None, "head"),
        P("head", None),
    )
    return jax.shard_map(
        local,
        mesh=mesh,
        in_specs=placed,
        out_specs=P(("groups", "seq", "sub"), "head"),
        check_vma=False,
    )
```

```python
import functools
import itertools
import math

import jax
import jax.numpy as jnp
import ml_dtypes
import numpy as np
from jax import lax
from jax.experimental import pallas as pl
from jax.experimental.pallas import tpu as pltpu
from jax.sharding import PartitionSpec as P

HDIM = 64
MEL = 128
NFFT = 512
HOP = 160
FP = 17
CH = 136
PE = 32

SAMPLE_RATE = 16000.0
EPSILON = 1e-05
MASKED = -1e30

LANES = 128
PIECE_BITS = 5
ROWS = 144
GROUP = 4
STACK = 4
MEL_WIDTH = FP * MEL
BF16 = jnp.bfloat16
F32 = jnp.float32


def split_bf16(values):
    high = values.astype(ml_dtypes.bfloat16)
    low = (values - high.astype(np.float64)).astype(ml_dtypes.bfloat16)
    return np.stack([high, low])


def fourier_tables():
    n, bins = np.arange(NFFT // 2)[:, None], NFFT // 2

    def phase(k):
        return 2.0 * np.pi * ((n * k[None, :]) % NFFT) / NFFT

    even, odd = np.arange(0, bins, 2), np.arange(1, bins, 2)
    sine = np.sin(phase(even))
    sine[:, 0] = np.cos(phase(np.array([bins])))[:, 0]
    return np.stack(
        [
            split_bf16(np.concatenate([np.cos(phase(even)), sine], axis=1)),
            split_bf16(np.concatenate([np.cos(phase(odd)), np.sin(phase(odd))], axis=1)),
        ]
    )


def window_halves():
    window = 0.5 - 0.5 * np.cos(2.0 * np.pi * np.arange(NFFT) / NFFT)
    return window.reshape(2, NFFT // 2).astype(np.float32)


def mel_tables():
    bins = NFFT // 2
    highest = 2595.0 * math.log10(1.0 + SAMPLE_RATE / 2.0 / 700.0)
    points = np.arange(MEL + 2) * (highest / (MEL + 1))
    hertz = 700.0 * (10.0 ** (points / 2595.0) - 1.0)
    centres = np.arange(bins + 1) * (SAMPLE_RATE / NFFT)
    rising = (centres[:, None] - hertz[None, :-2]) / (hertz[1:-1] - hertz[:-2])[None, :]
    falling = (hertz[None, 2:] - centres[:, None]) / (hertz[2:] - hertz[1:-1])[None, :]
    filters = np.maximum(0.0, np.minimum(rising, falling))
    filters = [filters[0:bins:2], filters[1:bins:2], filters[bins:], np.zeros((15, MEL))]
    high, low = split_bf16(np.concatenate(filters, axis=0))
    return np.concatenate([high, low], axis=1)


def dot(a, b):
    return jnp.dot(a, b, preferred_element_type=F32)


def iota(shape, dim):
    return lax.broadcasted_iota(jnp.int32, shape, dim)


def mel_kernel(shards, capacity, relative, *refs):
    sources, outs = refs[:5], refs[5:-6]
    targets, sems = refs[-6:-1], refs[-1]
    x_ref, target_ref, window_ref, fourier_ref, mel_ref = targets
    slots = x_ref.shape[0]
    pairs = zip(sources, targets)
    copies = [pltpu.make_async_copy(*pair, sems.at[k]) for k, pair in enumerate(pairs)]
    for copy in copies:
        copy.start()
    copies[1].wait()
    target = target_ref[...]
    owner = lax.shift_right_arithmetic(target, PIECE_BITS)
    place = jnp.where(target < 0, 0, (target & (PE - 1)) + 1).astype(F32)
    row, col = iota((slots, slots), 0), iota((slots, slots), 1)
    diagonal = row == col
    owner_col = jnp.sum(jnp.where(diagonal, owner, 0), axis=1, keepdims=True)
    place_col = jnp.sum(jnp.where(diagonal, place, 0.0), axis=1, keepdims=True)
    rank = jnp.sum(((owner_col == owner) & (row < col)).astype(jnp.int32), axis=0, keepdims=True)
    chosen = row // capacity
    if relative:
        chosen = chosen ^ lax.axis_index("seq")
    pick = ((chosen == owner) & (row % capacity == rank)).astype(F32).astype(BF16)
    marks = jnp.broadcast_to(place_col, (slots, LANES)).astype(BF16)

    copies[0].wait()
    copies[2].wait()
    x = x_ref[...]
    frames = [None] * FP
    half, bins = NFFT // 2, NFFT // 4
    rising, falling = window_ref[0:1, :], window_ref[1:2, :]
    later = iota((1, bins), 1) > 0
    for phase in range(4):
        shift = phase * (HOP % LANES)
        moved = x if phase == 0 else pltpu.roll(x, x.shape[1] - shift, 1)
        members = list(range(phase, FP, 4))
        sums, differences = [], []
        for f in members:
            start = HOP * f - shift
            left = moved[:, start : start + half] * rising
            right = moved[:, start + half : start + NFFT] * falling
            sums.append(left + right)
            differences.append(left - right)
        squares = []
        for k, parts in enumerate((sums, differences)):
            values = jnp.concatenate(parts, axis=0)
            high = values.astype(BF16)
            low = (values - high.astype(F32)).astype(BF16)
            if phase == 0 and k == 0:
                copies[3].wait()
            table_high, table_low = fourier_ref[k, 0], fourier_ref[k, 1]
            spectra = dot(
                jnp.concatenate([high, low, high], axis=1),
                jnp.concatenate([table_high, table_high, table_low], axis=0),
            )
            squares.append(spectra * spectra)
        if phase == 0:
            copies[4].wait()
            filters = mel_ref[:half, :]
            last_row = mel_ref[half:, :].astype(F32)
            last_row = last_row[:1, :MEL] + last_row[:1, MEL:]
        even, odd = squares
        last = even[:, bins : bins + 1] * last_row
        even = even[:, :bins] + jnp.where(later, even[:, bins:], 0.0)
        power = jnp.concatenate([even, odd[:, :bins] + odd[:, bins:]], axis=1)
        power_high = power.astype(BF16)
        power_low = (power - power_high.astype(F32)).astype(BF16)
        both = dot(
            jnp.concatenate([power_high, power_low], axis=1),
            jnp.concatenate([filters, filters], axis=0),
        )
        energy = both[:, :MEL] + both[:, MEL:] + last
        log_mel = jnp.log(1.0 + energy).astype(BF16)
        for k, f in enumerate(members):
            frames[f] = log_mel[k * slots : (k + 1) * slots]
    packed = dot(pick, jnp.concatenate(frames + [marks], axis=1)).astype(BF16)
    count = slots // len(outs)
    for d, out in enumerate(outs):
        out[...] = packed[d * count : (d + 1) * count]


def token_rows(pieces):
    groups = PE // GROUP
    rows = []
    for i in range(FP):
        cells = []
        for j in range(STACK):
            q, f = divmod(STACK * i + j, FP)
            cells.append(pieces[q * groups : (q + 1) * groups, f * MEL : (f + 1) * MEL])
        rows.append(jnp.concatenate(cells, axis=1))
    rows.append(jnp.zeros((ROWS - CH, STACK * MEL), F32))
    mixed = jnp.concatenate(rows, axis=0).astype(BF16)
    row, col = iota((ROWS, ROWS), 0), iota((ROWS, ROWS), 1)
    token = (col % groups) * FP + col // groups
    order = ((row == token) & (col < CH)).astype(F32).astype(BF16)
    return dot(order, mixed).astype(BF16)


def place_kernel(*refs):
    parts, out = refs[:-1], refs[-1]
    rows = jnp.concatenate([part[...] for part in parts], axis=0)
    slots = rows.shape[0]
    mark = rows[:, MEL_WIDTH : MEL_WIDTH + LANES].astype(F32)[:, :1]
    row, col = iota((slots, slots), 0), iota((slots, slots), 1)
    mark = jnp.sum(jnp.where(row == col, mark, 0.0), axis=0, keepdims=True)
    at = iota((PE, slots), 0)
    groups = PE // GROUP
    wanted = (at % groups) * GROUP + at // groups + 1
    pick = (wanted.astype(F32) == mark).astype(F32).astype(BF16)
    out[...] = token_rows(dot(pick, rows[:, :MEL_WIDTH]))


def prepare_kernel(
    lengths_hbm, table_hbm, qkv_hbm, out_ref, qkv_ref, lengths_ref, table_ref, flipped, sems
):
    copies = [
        pltpu.make_async_copy(lengths_hbm, lengths_ref, sems.at[0]),
        pltpu.make_async_copy(table_hbm, table_ref, sems.at[1]),
        pltpu.make_async_copy(qkv_hbm, qkv_ref, sems.at[2]),
    ]
    for copy in copies:
        copy.start()
    copies[0].wait()
    copies[1].wait()
    pairs, blocks = out_ref.shape[:2]
    half = blocks * CH
    first = (lax.axis_index("seq") * lax.axis_size("sub") + lax.axis_index("sub")) * half
    total = lax.axis_size("seq") * lax.axis_size("sub") * half
    lane, row = iota((1, 3 * ROWS), 1), iota((ROWS, 1), 0)
    orders = ((0, 1, 2), (2, 0, 1))
    slot = lane // ROWS
    key_place = lane - slot * ROWS
    masks = []
    for c in range(blocks):
        order = orders[1 if c == blocks - 1 else 0]
        key_block = jnp.where(slot == 0, order[0], jnp.where(slot == 1, order[1], order[2]))
        query = first + c * CH + row
        key = first + (c - 1) * CH + key_block * CH + key_place
        query_utt, key_utt = jnp.zeros_like(query), jnp.zeros_like(key)
        end = jnp.int32(0)
        for r in range(lengths_ref.shape[0]):
            end = end + lengths_ref[r]
            query_utt = query_utt + (query >= end).astype(jnp.int32)
            key_utt = key_utt + (key >= end).astype(jnp.int32)
        inside = (key >= 0) & (key < total) & (key_place < CH)
        key_utt = jnp.where(inside, key_utt, -1)
        masks.append(jnp.where(query_utt == key_utt, 0.0, MASKED))
    heads, entries = table_ref.shape
    width = flipped.shape[1]
    mirror = iota((entries, width), 0) + iota((entries, width), 1) == entries - 1
    mirror = mirror.astype(F32).astype(BF16)
    rest, lines = table_ref[...], 0.0
    for _ in range(3):
        part = rest.astype(BF16)
        rest = rest - part.astype(F32)
        lines = lines + dot(part, mirror)
    flipped[...] = lines

    def one_head(head, side):
        line = jnp.broadcast_to(flipped[pl.ds(head, 1), :], (ROWS, width))
        biases = []
        for order in orders:
            turned = [
                pltpu.roll(
                    line, (ROWS * at - CH * b - (CH - 1)) % width, 1, stride=1, stride_axis=0
                )[:, : 3 * ROWS]
                for at, b in enumerate(order)
            ]
            biases.append(
                jnp.where(slot == 0, turned[0], jnp.where(slot == 1, turned[1], turned[2]))
            )
        for c in range(blocks):
            bias = biases[1 if c == blocks - 1 else 0]
            out_ref[head // 2, c, side * ROWS : (side + 1) * ROWS, :] = bias + masks[c]

    @pl.loop(0, pairs)
    def _(pair):
        one_head(2 * pair, 0)
        one_head(2 * pair + 1, 1)

    copies[2].wait()


def normalize(tokens, conv, conv_bias, gain, out):
    summed = dot(tokens, conv[...]) + conv_bias[...]
    half = 0.5 * summed
    features = (half + half * jnp.tanh(half)).astype(BF16).astype(F32)
    scale = 1.0 / features.shape[1]
    centred = features - jnp.sum(features, axis=1, keepdims=True) * scale
    variance = jnp.sum(centred * centred, axis=1, keepdims=True) * scale
    out[...] = (centred * lax.rsqrt(variance + EPSILON) * gain[...]).astype(BF16)


def own_kernel(n, *refs):
    pieces, parts, refs = refs[0], refs[1 : 2 * n], refs[2 * n :]
    bias_parts, gain_rows, refs = refs[:n], refs[n], refs[n + 1 :]
    qkv, q_out, k_out, v_out, conv, conv_bias, gain, normed = refs
    me, core = lax.axis_index("head"), lax.axis_index("sub")
    depth = parts[0].shape[1]
    for d in range(n):
        start = pl.multiple_of(lax.rem(me + d, n) * depth, depth)
        at = pl.ds(start, depth)
        lines = bias_parts[d][...].astype(F32)
        for k in range(depth // LANES):
            conv_bias[:, pl.ds(start + k * LANES, LANES)] = lines[k : k + 1]
        if d == 0:
            conv[:, at] = parts[0][...]
        else:
            got, swapped = parts[2 * d - 1 : 2 * d + 1]

            @pl.when(core == 0)
            def _(got=got, at=at):
                conv[:, at] = got[...]

            @pl.when(core == 1)
            def _(swapped=swapped, at=at):
                conv[:, at] = swapped[...]

    for k in range(gain_rows.shape[0]):
        gain[:, k * LANES : (k + 1) * LANES] = gain_rows[k : k + 1, :]
    normalize(pieces[...], conv, conv_bias, gain, normed)
    for p, out in enumerate((q_out, k_out, v_out)):
        out[0] = dot(normed[...], qkv[p]).astype(BF16)


def others_kernel(n, *refs):
    own, pieces = refs[:3], refs[3 : n + 2]
    conv, conv_bias, gain, qkv, *outs, sent, normed = refs[n + 2 :]
    me, core = lax.axis_index("head"), lax.axis_index("sub")
    tokens = jnp.concatenate([piece[...] for piece in pieces], axis=0)
    normalize(tokens, conv, conv_bias, gain, normed)
    wanted = jnp.where(core == 0, n - 1, 0)
    for p, (source, out) in enumerate(zip(own, outs)):
        out[me] = source[0]
        got = dot(normed[...], qkv[p]).astype(BF16)
        for d in range(1, n):
            out[lax.rem(me + d, n)] = got[(d - 1) * ROWS : d * ROWS]
        if p > 0:
            sent[p - 1] = out[wanted]


def attend(q, k, v, bias):
    low_lanes = iota((ROWS, LANES), 1) < HDIM
    q = q * jnp.asarray(1.0 / math.sqrt(HDIM), BF16)
    zero = jnp.zeros_like(q)
    q = jnp.concatenate([jnp.where(low_lanes, q, zero), jnp.where(low_lanes, zero, q)], axis=0)
    scores = lax.dot_general(q, k, (((1,), (1,)), ((), ())), preferred_element_type=F32) + bias
    weights = jnp.exp(scores - jnp.max(scores, axis=1, keepdims=True)).astype(BF16)
    summed = dot(weights, jnp.concatenate([v, jnp.ones_like(v)], axis=1))
    context = summed[:, :LANES] * (1.0 / summed[:, LANES:])
    return jnp.where(low_lanes, context[:ROWS], context[ROWS:])


def edge_context(pair, block, halo_keys, halo_values, first, queries, keys, values, bias):
    at = slice(pair * LANES, (pair + 1) * LANES)
    return attend(
        queries[block, :, at],
        jnp.concatenate([halo_keys[:, at], keys[first, :, at], keys[first + 1, :, at]], axis=0),
        jnp.concatenate(
            [halo_values[:, at], values[first, :, at], values[first + 1, :, at]], axis=0
        ),
        bias[pair, block],
    )


def far_kernel(n, *refs):
    (queries, keys, values), rounds, refs = refs[:3], refs[3 : n + 3], refs[n + 3 :]
    conv, conv_bias, gain, qkv, bias, out, normed, far_keys, far_values = refs
    me, core = lax.axis_index("head"), lax.axis_index("sub")
    far, turn = rounds[0][...], jnp.where(core == 0, n - 1 - me, me)
    for r in range(1, n):
        far = jnp.where(turn == r, rounds[r][...], far)
    normalize(far, conv, conv_bias, gain, normed)
    far_keys[...] = dot(normed[...], qkv[1]).astype(BF16)
    far_values[...] = dot(normed[...], qkv[2]).astype(BF16)
    block, first = jnp.where(core == 0, 0, n - 1), jnp.where(core == 0, 0, n - 2)
    for pair in range(qkv.shape[2] // LANES):
        context = edge_context(
            pair, block, far_keys, far_values, first, queries, keys, values, bias
        )
        out[:, pair * LANES : (pair + 1) * LANES] = context.astype(BF16)


def near_kernel(n, *refs):
    queries, keys, values, near, far_context, bias, out_hbm, out, sems = refs
    core = lax.axis_index("sub")
    copies = []
    block, first = jnp.where(core == 0, n - 1, 0), jnp.where(core == 0, n - 2, 0)
    for pair in range(queries.shape[2] // LANES):
        at = slice(pair * LANES, (pair + 1) * LANES)
        context = edge_context(
            pair, block, near.at[0], near.at[1], first, queries, keys, values, bias
        )[:CH]
        middle = [
            attend(
                queries[c, :, at],
                keys[c - 1 : c + 2, :, at].reshape(3 * ROWS, LANES),
                values[c - 1 : c + 2, :, at].reshape(3 * ROWS, LANES),
                bias[pair, c],
            )[:CH]
            for c in range(1, n - 1)
        ]
        other = far_context[:, at].astype(F32)[:CH]
        out[:, at] = jnp.where(
            core == 0,
            jnp.concatenate([other] + middle + [context], axis=0),
            jnp.concatenate([context] + middle + [other], axis=0),
        ).astype(BF16)
        copies.append(pltpu.make_async_copy(out.at[:, at], out_hbm.at[:, at], sems.at[pair]))
        copies[-1].start()
    for copy in copies:
        copy.wait()


def vmem(count):
    return [pl.BlockSpec(memory_space=pltpu.VMEM)] * count


def from_hbm(array):
    return pltpu.with_memory_space_constraint(array, pltpu.HBM)


def in_vmem(array):
    return pltpu.with_memory_space_constraint(array, pltpu.VMEM)


def from_heads(block, n):
    return [lax.ppermute(block, "head", [((i + d) % n, i) for i in range(n)]) for d in range(1, n)]


def local(
    wave_pieces, piece_target, utt_lengths, sub_weight, sub_bias, norm_gain, qkv_weight, rel_bias
):
    shards, n, cores = lax.axis_size("seq"), lax.axis_size("head"), lax.axis_size("sub")
    assert cores == 2
    slots, length = wave_pieces.shape[3:]
    capacity = slots // shards
    relative = shards in (2, 4) and capacity % 16 == 0
    outs = shards if relative else 1
    payload = MEL_WIDTH + LANES
    fourier, filters, window = fourier_tables(), mel_tables(), window_halves()
    in_hbm = pl.BlockSpec(memory_space=pltpu.HBM)
    groups = lax.axis_size("groups")
    weight_got, bias_got = [], from_heads(sub_bias, n)
    for d in range(1, n):
        links = []
        for g in range(groups):
            for h in range(n):
                at = (g * n + h) * cores
                links.append(((g * n + (h + d) % n) * cores, at))
                links.append((((g + 1) % groups * n + h) * cores + 1, at + 1))
        weight_got.append(lax.ppermute(sub_weight, ("groups", "head", "sub"), links))
    packed = pl.pallas_call(
        functools.partial(mel_kernel, shards, capacity, relative),
        out_shape=[jax.ShapeDtypeStruct((slots // outs, payload), BF16)] * outs,
        in_specs=[in_hbm] * 5,
        out_specs=vmem(outs),
        scratch_shapes=[
            pltpu.VMEM((slots, length), F32),
            pltpu.VMEM((1, slots), jnp.int32),
            pltpu.VMEM(window.shape, F32),
            pltpu.VMEM(fourier.shape, BF16),
            pltpu.VMEM(filters.shape, BF16),
            pltpu.SemaphoreType.DMA((5,)),
        ],
        compiler_params=pltpu.CompilerParams(vmem_limit_bytes=24 << 20),
        name="log_mel",
    )(
        from_hbm(wave_pieces.reshape(slots, length)),
        from_hbm(piece_target.reshape(1, slots)),
        from_hbm(jnp.asarray(window)),
        from_hbm(jnp.asarray(fourier)),
        from_hbm(jnp.asarray(filters)),
    )
    if relative:
        received = [
            lax.ppermute(packed[d], "seq", [(i, i ^ d) for i in range(shards)])
            for d in range(shards - 1, 0, -1)
        ] + [packed[0]]
    else:
        blocks = packed[0].reshape(shards, capacity, payload)
        blocks = lax.all_to_all(blocks, "seq", split_axis=0, concat_axis=0, tiled=True)
        received = [blocks.reshape(slots, payload)]

    local_width = qkv_weight.shape[2]
    pairs = local_width // LANES
    gain = norm_gain.reshape(-1, LANES)
    rel_bias, gain, _ = lax.optimization_barrier((rel_bias, gain, packed[0]))
    entries = rel_bias.shape[1]
    qkv = jnp.transpose(qkv_weight, (1, 0, 2))
    bias, qkv = pl.pallas_call(
        prepare_kernel,
        out_shape=[
            pltpu.VMEM((pairs, n, 2 * ROWS, 3 * ROWS), F32),
            pltpu.VMEM(qkv.shape, BF16),
        ],
        in_specs=[in_hbm] * 3,
        out_specs=vmem(2),
        scratch_shapes=[
            pltpu.SMEM(utt_lengths.shape, jnp.int32),
            pltpu.VMEM(rel_bias.shape, F32),
            pltpu.VMEM((2 * pairs, entries + -entries % LANES), F32),
            pltpu.SemaphoreType.DMA((3,)),
        ],
        compiler_params=pltpu.CompilerParams(vmem_limit_bytes=8 << 20),
        cost_estimate=pl.CostEstimate(flops=1 << 31, bytes_accessed=8 << 20, transcendentals=0),
        name="prepare",
    )(from_hbm(utt_lengths), from_hbm(rel_bias), from_hbm(qkv))
    received, weight_got, bias_got, bias, qkv, gain = lax.optimization_barrier(
        (received, weight_got, bias_got, bias, qkv, gain)
    )
    own = pl.pallas_call(
        place_kernel,
        out_shape=jax.ShapeDtypeStruct((ROWS, STACK * MEL), BF16),
        in_specs=vmem(len(received)),
        out_specs=vmem(1)[0],
        compiler_params=pltpu.CompilerParams(vmem_limit_bytes=8 << 20),
        name="place",
    )(*received)
    conv = [sub_weight]
    for got in weight_got:
        got, _ = lax.optimization_barrier((got, own))
        conv += [got, lax.ppermute(got, "sub", [(0, 1), (1, 0)])]
    conv_bias = [line.reshape(-1, LANES) for line in [sub_bias] + bias_got]

    others = from_heads(own, n)
    width = qkv_weight.shape[0]
    qkv = in_vmem(qkv)
    limit = pltpu.CompilerParams(vmem_limit_bytes=16 << 20)
    rounds = [None] * n
    for r in reversed(range(n)):
        links = {}
        for g in range(groups):
            for k in range(shards - 1):
                for source, target in (
                    ((g, k, n - 1, 1), (g, k + 1, r, 0)),
                    ((g, k + 1, 0, 0), (g, k, n - 1 - r, 1)),
                ):
                    links[source] = target
        for source, target in list(links.items()):
            links.setdefault(target, source)
        for g in range(groups):
            for end in ((g, 0, 0, 0), (g, shards - 1, n - 1, 1)):
                beside = (*end[:2], n - 1 - end[2], end[3])
                if end not in links and beside not in links:
                    links.update({end: beside, beside: end} if r == 0 else {})
        for place in itertools.product(range(groups), range(shards), range(n), range(cores)):
            links.setdefault(place, ((place[0] + 1) % groups, *place[1:]))
        assert len(set(links.values())) == len(links)
        sizes = (groups, shards, n, cores)
        flat = [tuple(int(np.ravel_multi_index(p, sizes)) for p in link) for link in links.items()]
        rounds[r] = lax.ppermute(own, ("groups", "seq", "head", "sub"), flat)
    limit = pltpu.CompilerParams(vmem_limit_bytes=16 << 20)
    *own_qkv, whole, whole_bias, whole_gain = pl.pallas_call(
        functools.partial(own_kernel, n),
        out_shape=[jax.ShapeDtypeStruct((1, ROWS, local_width), BF16)] * 3
        + [
            jax.ShapeDtypeStruct((sub_weight.shape[0], width), BF16),
            jax.ShapeDtypeStruct((1, width), F32),
            jax.ShapeDtypeStruct((1, width), F32),
        ],
        in_specs=vmem(1 + len(conv) + len(conv_bias) + 2),
        out_specs=vmem(6),
        scratch_shapes=[pltpu.VMEM((ROWS, width), BF16)],
        compiler_params=limit,
        cost_estimate=pl.CostEstimate(flops=1 << 20, bytes_accessed=1 << 20, transcendentals=0),
        name="own",
    )(own, *conv, *conv_bias, gain, qkv)
    weights = (whole, whole_bias, whole_gain, qkv)
    *half_qkv, near_sent = pl.pallas_call(
        functools.partial(others_kernel, n),
        out_shape=[jax.ShapeDtypeStruct((n, ROWS, local_width), BF16)] * 3
        + [jax.ShapeDtypeStruct((2, ROWS, local_width), BF16)],
        in_specs=vmem(n + 2 + len(weights)),
        out_specs=vmem(4),
        scratch_shapes=[pltpu.VMEM(((n - 1) * ROWS, width), BF16)],
        compiler_params=limit,
        cost_estimate=pl.CostEstimate(flops=4 << 30, bytes_accessed=9 << 20, transcendentals=0),
        name="others",
    )(*own_qkv, *others, *weights)
    near = lax.ppermute(near_sent, "sub", [(0, 1), (1, 0)])
    far_context = pl.pallas_call(
        functools.partial(far_kernel, n),
        out_shape=jax.ShapeDtypeStruct((ROWS, local_width), BF16),
        in_specs=vmem(3 + n + len(weights) + 1),
        out_specs=vmem(1)[0],
        scratch_shapes=[
            pltpu.VMEM((ROWS, width), BF16),
            pltpu.VMEM((ROWS, local_width), BF16),
            pltpu.VMEM((ROWS, local_width), BF16),
        ],
        compiler_params=limit,
        cost_estimate=pl.CostEstimate(flops=16 << 30, bytes_accessed=9 << 20, transcendentals=0),
        name="far",
    )(*half_qkv, *rounds[::-1], *weights, in_vmem(bias))
    return pl.pallas_call(
        functools.partial(near_kernel, n),
        out_shape=jax.ShapeDtypeStruct((n * CH, local_width), BF16),
        in_specs=vmem(6),
        out_specs=in_hbm,
        scratch_shapes=[
            pltpu.VMEM((n * CH, local_width), BF16),
            pltpu.SemaphoreType.DMA((pairs,)),
        ],
        compiler_params=limit,
        name="near",
    )(*half_qkv, near, far_context, in_vmem(bias))


def solution(mesh):
    placed = (
        P(("groups", "seq"), "head", "sub", None, None),
        P(("groups", "seq"), "head", "sub", None),
        P("groups"),
        P(None, "head"),
        P("head"),
        P(),
        P(None, None, "head"),
        P("head", None),
    )
    return jax.shard_map(
        local,
        mesh=mesh,
        in_specs=placed,
        out_specs=P(("groups", "seq", "sub"), "head"),
        check_vma=False,
    )
```

```python
import functools
import itertools
import math

import jax
import jax.numpy as jnp
import ml_dtypes
import numpy as np
from jax import lax
from jax.experimental import pallas as pl
from jax.experimental.pallas import tpu as pltpu
from jax.sharding import PartitionSpec as P

HDIM = 64
MEL = 128
NFFT = 512
HOP = 160
FP = 17
CH = 136
PE = 32

SAMPLE_RATE = 16000.0
EPSILON = 1e-05
MASKED = -1e30

LANES = 128
PIECE_BITS = 5
ROWS = 144
GROUP = 4
STACK = 4
MEL_WIDTH = FP * MEL
BF16 = jnp.bfloat16
F32 = jnp.float32


def split_bf16(values):
    high = values.astype(ml_dtypes.bfloat16)
    low = (values - high.astype(np.float64)).astype(ml_dtypes.bfloat16)
    return np.stack([high, low])


def fourier_tables():
    n, bins = np.arange(NFFT // 2)[:, None], NFFT // 2

    def phase(k):
        return 2.0 * np.pi * ((n * k[None, :]) % NFFT) / NFFT

    even, odd = np.arange(0, bins, 2), np.arange(1, bins, 2)
    sine = np.sin(phase(even))
    sine[:, 0] = np.cos(phase(np.array([bins])))[:, 0]
    return np.stack(
        [
            split_bf16(np.concatenate([np.cos(phase(even)), sine], axis=1)),
            split_bf16(np.concatenate([np.cos(phase(odd)), np.sin(phase(odd))], axis=1)),
        ]
    )


def window_halves():
    window = 0.5 - 0.5 * np.cos(2.0 * np.pi * np.arange(NFFT) / NFFT)
    return window.reshape(2, NFFT // 2).astype(np.float32)


def mel_tables():
    bins = NFFT // 2
    highest = 2595.0 * math.log10(1.0 + SAMPLE_RATE / 2.0 / 700.0)
    points = np.arange(MEL + 2) * (highest / (MEL + 1))
    hertz = 700.0 * (10.0 ** (points / 2595.0) - 1.0)
    centres = np.arange(bins + 1) * (SAMPLE_RATE / NFFT)
    rising = (centres[:, None] - hertz[None, :-2]) / (hertz[1:-1] - hertz[:-2])[None, :]
    falling = (hertz[None, 2:] - centres[:, None]) / (hertz[2:] - hertz[1:-1])[None, :]
    filters = np.maximum(0.0, np.minimum(rising, falling))
    filters = [filters[0:bins:2], filters[1:bins:2], filters[bins:], np.zeros((15, MEL))]
    high, low = split_bf16(np.concatenate(filters, axis=0))
    return np.concatenate([high, low], axis=1)


def dot(a, b):
    return jnp.dot(a, b, preferred_element_type=F32)


def iota(shape, dim):
    return lax.broadcasted_iota(jnp.int32, shape, dim)


def mel_kernel(shards, capacity, relative, *refs):
    sources, outs = refs[:5], refs[5:-6]
    targets, sems = refs[-6:-1], refs[-1]
    x_ref, target_ref, window_ref, fourier_ref, mel_ref = targets
    slots = x_ref.shape[0]
    pairs = zip(sources, targets)
    copies = [pltpu.make_async_copy(*pair, sems.at[k]) for k, pair in enumerate(pairs)]
    for copy in copies:
        copy.start()
    copies[1].wait()
    target = target_ref[...]
    owner = lax.shift_right_arithmetic(target, PIECE_BITS)
    place = jnp.where(target < 0, 0, (target & (PE - 1)) + 1).astype(F32)
    row, col = iota((slots, slots), 0), iota((slots, slots), 1)
    diagonal = row == col
    owner_col = jnp.sum(jnp.where(diagonal, owner, 0), axis=1, keepdims=True)
    place_col = jnp.sum(jnp.where(diagonal, place, 0.0), axis=1, keepdims=True)
    rank = jnp.sum(((owner_col == owner) & (row < col)).astype(jnp.int32), axis=0, keepdims=True)
    chosen = row // capacity
    if relative:
        chosen = chosen ^ lax.axis_index("seq")
    pick = ((chosen == owner) & (row % capacity == rank)).astype(F32).astype(BF16)
    marks = jnp.broadcast_to(place_col, (slots, LANES)).astype(BF16)

    copies[0].wait()
    copies[2].wait()
    x = x_ref[...]
    frames = [None] * FP
    half, bins = NFFT // 2, NFFT // 4
    rising, falling = window_ref[0:1, :], window_ref[1:2, :]
    later = iota((1, bins), 1) > 0
    for phase in range(4):
        shift = phase * (HOP % LANES)
        moved = x if phase == 0 else pltpu.roll(x, x.shape[1] - shift, 1)
        members = list(range(phase, FP, 4))
        sums, differences = [], []
        for f in members:
            start = HOP * f - shift
            left = moved[:, start : start + half] * rising
            right = moved[:, start + half : start + NFFT] * falling
            sums.append(left + right)
            differences.append(left - right)
        squares = []
        for k, parts in enumerate((sums, differences)):
            values = jnp.concatenate(parts, axis=0)
            high = values.astype(BF16)
            low = (values - high.astype(F32)).astype(BF16)
            if phase == 0 and k == 0:
                copies[3].wait()
            table_high, table_low = fourier_ref[k, 0], fourier_ref[k, 1]
            spectra = dot(
                jnp.concatenate([high, low, high], axis=1),
                jnp.concatenate([table_high, table_high, table_low], axis=0),
            )
            squares.append(spectra * spectra)
        if phase == 0:
            copies[4].wait()
            filters = mel_ref[:half, :]
            last_row = mel_ref[half:, :].astype(F32)
            last_row = last_row[:1, :MEL] + last_row[:1, MEL:]
        even, odd = squares
        last = even[:, bins : bins + 1] * last_row
        even = even[:, :bins] + jnp.where(later, even[:, bins:], 0.0)
        power = jnp.concatenate([even, odd[:, :bins] + odd[:, bins:]], axis=1)
        power_high = power.astype(BF16)
        power_low = (power - power_high.astype(F32)).astype(BF16)
        both = dot(
            jnp.concatenate([power_high, power_low], axis=1),
            jnp.concatenate([filters, filters], axis=0),
        )
        energy = both[:, :MEL] + both[:, MEL:] + last
        log_mel = jnp.log(1.0 + energy).astype(BF16)
        for k, f in enumerate(members):
            frames[f] = log_mel[k * slots : (k + 1) * slots]
    packed = dot(pick, jnp.concatenate(frames + [marks], axis=1)).astype(BF16)
    count = slots // len(outs)
    for d, out in enumerate(outs):
        out[...] = packed[d * count : (d + 1) * count]


def token_rows(pieces):
    groups = PE // GROUP
    rows = []
    for i in range(FP):
        cells = []
        for j in range(STACK):
            q, f = divmod(STACK * i + j, FP)
            cells.append(pieces[q * groups : (q + 1) * groups, f * MEL : (f + 1) * MEL])
        rows.append(jnp.concatenate(cells, axis=1))
    rows.append(jnp.zeros((ROWS - CH, STACK * MEL), F32))
    mixed = jnp.concatenate(rows, axis=0).astype(BF16)
    row, col = iota((ROWS, ROWS), 0), iota((ROWS, ROWS), 1)
    token = (col % groups) * FP + col // groups
    order = ((row == token) & (col < CH)).astype(F32).astype(BF16)
    return dot(order, mixed).astype(BF16)


def place_kernel(*refs):
    parts, out = refs[:-1], refs[-1]
    rows = jnp.concatenate([part[...] for part in parts], axis=0)
    slots = rows.shape[0]
    mark = rows[:, MEL_WIDTH : MEL_WIDTH + LANES].astype(F32)[:, :1]
    row, col = iota((slots, slots), 0), iota((slots, slots), 1)
    mark = jnp.sum(jnp.where(row == col, mark, 0.0), axis=0, keepdims=True)
    at = iota((PE, slots), 0)
    groups = PE // GROUP
    wanted = (at % groups) * GROUP + at // groups + 1
    pick = (wanted.astype(F32) == mark).astype(F32).astype(BF16)
    out[...] = token_rows(dot(pick, rows[:, :MEL_WIDTH]))


def prepare_kernel(
    lengths_hbm, table_hbm, qkv_hbm, out_ref, qkv_ref, lengths_ref, table_ref, flipped, sems
):
    copies = [
        pltpu.make_async_copy(lengths_hbm, lengths_ref, sems.at[0]),
        pltpu.make_async_copy(table_hbm, table_ref, sems.at[1]),
        pltpu.make_async_copy(qkv_hbm, qkv_ref, sems.at[2]),
    ]
    for copy in copies:
        copy.start()
    copies[0].wait()
    copies[1].wait()
    pairs, blocks = out_ref.shape[:2]
    half = blocks * CH
    first = (lax.axis_index("seq") * lax.axis_size("sub") + lax.axis_index("sub")) * half
    total = lax.axis_size("seq") * lax.axis_size("sub") * half
    lane, row = iota((1, 3 * ROWS), 1), iota((ROWS, 1), 0)
    orders = ((0, 1, 2), (2, 0, 1))
    slot = lane // ROWS
    key_place = lane - slot * ROWS
    masks = []
    for c in range(blocks):
        order = orders[1 if c == blocks - 1 else 0]
        key_block = jnp.where(slot == 0, order[0], jnp.where(slot == 1, order[1], order[2]))
        query = first + c * CH + row
        key = first + (c - 1) * CH + key_block * CH + key_place
        query_utt, key_utt = jnp.zeros_like(query), jnp.zeros_like(key)
        end = jnp.int32(0)
        for r in range(lengths_ref.shape[0]):
            end = end + lengths_ref[r]
            query_utt = query_utt + (query >= end).astype(jnp.int32)
            key_utt = key_utt + (key >= end).astype(jnp.int32)
        inside = (key >= 0) & (key < total) & (key_place < CH)
        key_utt = jnp.where(inside, key_utt, -1)
        masks.append(jnp.where(query_utt == key_utt, 0.0, MASKED))
    heads, entries = table_ref.shape
    width = flipped.shape[1]
    mirror = iota((entries, width), 0) + iota((entries, width), 1) == entries - 1
    mirror = mirror.astype(F32).astype(BF16)
    rest, lines = table_ref[...], 0.0
    for _ in range(3):
        part = rest.astype(BF16)
        rest = rest - part.astype(F32)
        lines = lines + dot(part, mirror)
    flipped[...] = lines

    def one_head(head, side):
        line = jnp.broadcast_to(flipped[pl.ds(head, 1), :], (ROWS, width))
        biases = []
        for order in orders:
            turned = [
                pltpu.roll(
                    line, (ROWS * at - CH * b - (CH - 1)) % width, 1, stride=1, stride_axis=0
                )[:, : 3 * ROWS]
                for at, b in enumerate(order)
            ]
            biases.append(
                jnp.where(slot == 0, turned[0], jnp.where(slot == 1, turned[1], turned[2]))
            )
        for c in range(blocks):
            bias = biases[1 if c == blocks - 1 else 0]
            out_ref[head // 2, c, side * ROWS : (side + 1) * ROWS, :] = bias + masks[c]

    @pl.loop(0, pairs)
    def _(pair):
        one_head(2 * pair, 0)
        one_head(2 * pair + 1, 1)

    copies[2].wait()


def normalize(tokens, conv, conv_bias, gain, out):
    summed = dot(tokens, conv[...]) + conv_bias[...]
    half = 0.5 * summed
    features = (half + half * jnp.tanh(half)).astype(BF16).astype(F32)
    scale = 1.0 / features.shape[1]
    centred = features - jnp.sum(features, axis=1, keepdims=True) * scale
    variance = jnp.sum(centred * centred, axis=1, keepdims=True) * scale
    out[...] = (centred * lax.rsqrt(variance + EPSILON) * gain[...]).astype(BF16)


def own_kernel(n, *refs):
    pieces, parts, refs = refs[0], refs[1 : 2 * n], refs[2 * n :]
    bias_parts, gain_rows, refs = refs[:n], refs[n], refs[n + 1 :]
    qkv, q_out, k_out, v_out, conv, conv_bias, gain, normed = refs
    me, core = lax.axis_index("head"), lax.axis_index("sub")
    depth = parts[0].shape[1]
    for d in range(n):
        start = pl.multiple_of(lax.rem(me + d, n) * depth, depth)
        at = pl.ds(start, depth)
        lines = bias_parts[d][...].astype(F32)
        for k in range(depth // LANES):
            conv_bias[:, pl.ds(start + k * LANES, LANES)] = lines[k : k + 1]
        if d == 0:
            conv[:, at] = parts[0][...]
        else:
            got, swapped = parts[2 * d - 1 : 2 * d + 1]

            @pl.when(core == 0)
            def _(got=got, at=at):
                conv[:, at] = got[...]

            @pl.when(core == 1)
            def _(swapped=swapped, at=at):
                conv[:, at] = swapped[...]

    for k in range(gain_rows.shape[0]):
        gain[:, k * LANES : (k + 1) * LANES] = gain_rows[k : k + 1, :]
    normalize(pieces[...], conv, conv_bias, gain, normed)
    for p, out in enumerate((q_out, k_out, v_out)):
        out[0] = dot(normed[...], qkv[p]).astype(BF16)


def others_kernel(n, *refs):
    own, pieces = refs[:3], refs[3 : n + 2]
    conv, conv_bias, gain, qkv, *outs, sent, normed = refs[n + 2 :]
    me, core = lax.axis_index("head"), lax.axis_index("sub")
    tokens = jnp.concatenate([piece[...] for piece in pieces], axis=0)
    normalize(tokens, conv, conv_bias, gain, normed)
    wanted = jnp.where(core == 0, n - 1, 0)
    for p, (source, out) in enumerate(zip(own, outs)):
        out[me] = source[0]
        got = dot(normed[...], qkv[p]).astype(BF16)
        for d in range(1, n):
            out[lax.rem(me + d, n)] = got[(d - 1) * ROWS : d * ROWS]
        if p > 0:
            sent[p - 1] = out[wanted]


def attend(q, k, v, bias):
    low_lanes = iota((ROWS, LANES), 1) < HDIM
    q = q * jnp.asarray(1.0 / math.sqrt(HDIM), BF16)
    zero = jnp.zeros_like(q)
    q = jnp.concatenate([jnp.where(low_lanes, q, zero), jnp.where(low_lanes, zero, q)], axis=0)
    scores = lax.dot_general(q, k, (((1,), (1,)), ((), ())), preferred_element_type=F32) + bias
    weights = jnp.exp(scores - jnp.max(scores, axis=1, keepdims=True)).astype(BF16)
    summed = dot(weights, jnp.concatenate([v, jnp.ones_like(v)], axis=1))
    context = summed[:, :LANES] * (1.0 / summed[:, LANES:])
    return jnp.where(low_lanes, context[:ROWS], context[ROWS:])


def edge_context(pair, block, halo_keys, halo_values, first, queries, keys, values, bias):
    at = slice(pair * LANES, (pair + 1) * LANES)
    return attend(
        queries[block, :, at],
        jnp.concatenate([halo_keys[:, at], keys[first, :, at], keys[first + 1, :, at]], axis=0),
        jnp.concatenate(
            [halo_values[:, at], values[first, :, at], values[first + 1, :, at]], axis=0
        ),
        bias[pair, block],
    )


def far_kernel(n, *refs):
    (queries, keys, values), rounds, refs = refs[:3], refs[3 : n + 3], refs[n + 3 :]
    conv, conv_bias, gain, qkv, bias, out, normed, far_keys, far_values = refs
    me, core = lax.axis_index("head"), lax.axis_index("sub")
    far, turn = rounds[0][...], jnp.where(core == 0, n - 1 - me, me)
    for r in range(1, n):
        far = jnp.where(turn == r, rounds[r][...], far)
    normalize(far, conv, conv_bias, gain, normed)
    far_keys[...] = dot(normed[...], qkv[1]).astype(BF16)
    far_values[...] = dot(normed[...], qkv[2]).astype(BF16)
    block, first = jnp.where(core == 0, 0, n - 1), jnp.where(core == 0, 0, n - 2)
    for pair in range(qkv.shape[2] // LANES):
        context = edge_context(
            pair, block, far_keys, far_values, first, queries, keys, values, bias
        )
        out[:, pair * LANES : (pair + 1) * LANES] = context.astype(BF16)


def near_kernel(n, *refs):
    queries, keys, values, near, far_context, bias, out_hbm, out, sems = refs
    core = lax.axis_index("sub")
    copies = []
    block, first = jnp.where(core == 0, n - 1, 0), jnp.where(core == 0, n - 2, 0)
    for pair in range(queries.shape[2] // LANES):
        at = slice(pair * LANES, (pair + 1) * LANES)
        context = edge_context(
            pair, block, near.at[0], near.at[1], first, queries, keys, values, bias
        )[:CH]
        middle = [
            attend(
                queries[c, :, at],
                keys[c - 1 : c + 2, :, at].reshape(3 * ROWS, LANES),
                values[c - 1 : c + 2, :, at].reshape(3 * ROWS, LANES),
                bias[pair, c],
            )[:CH]
            for c in range(1, n - 1)
        ]
        other = far_context[:, at].astype(F32)[:CH]
        out[:, at] = jnp.where(
            core == 0,
            jnp.concatenate([other] + middle + [context], axis=0),
            jnp.concatenate([context] + middle + [other], axis=0),
        ).astype(BF16)
        copies.append(pltpu.make_async_copy(out.at[:, at], out_hbm.at[:, at], sems.at[pair]))
        copies[-1].start()
    for copy in copies:
        copy.wait()


def vmem(count):
    return [pl.BlockSpec(memory_space=pltpu.VMEM)] * count


def from_hbm(array):
    return pltpu.with_memory_space_constraint(array, pltpu.HBM)


def in_vmem(array):
    return pltpu.with_memory_space_constraint(array, pltpu.VMEM)


def from_heads(block, n):
    return [lax.ppermute(block, "head", [((i + d) % n, i) for i in range(n)]) for d in range(1, n)]


def local(
    wave_pieces, piece_target, utt_lengths, sub_weight, sub_bias, norm_gain, qkv_weight, rel_bias
):
    shards, n, cores = lax.axis_size("seq"), lax.axis_size("head"), lax.axis_size("sub")
    assert cores == 2
    slots, length = wave_pieces.shape[3:]
    capacity = slots // shards
    relative = shards in (2, 4) and capacity % 16 == 0
    outs = shards if relative else 1
    payload = MEL_WIDTH + LANES
    fourier, filters, window = fourier_tables(), mel_tables(), window_halves()
    in_hbm = pl.BlockSpec(memory_space=pltpu.HBM)
    groups = lax.axis_size("groups")
    weight_got, bias_got = [], from_heads(sub_bias, n)
    for d in range(1, n):
        links = []
        for g in range(groups):
            for h in range(n):
                at = (g * n + h) * cores
                links.append(((g * n + (h + d) % n) * cores, at))
                links.append((((g + 1) % groups * n + h) * cores + 1, at + 1))
        weight_got.append(lax.ppermute(sub_weight, ("groups", "head", "sub"), links))
    packed = pl.pallas_call(
        functools.partial(mel_kernel, shards, capacity, relative),
        out_shape=[jax.ShapeDtypeStruct((slots // outs, payload), BF16)] * outs,
        in_specs=[in_hbm] * 5,
        out_specs=vmem(outs),
        scratch_shapes=[
            pltpu.VMEM((slots, length), F32),
            pltpu.VMEM((1, slots), jnp.int32),
            pltpu.VMEM(window.shape, F32),
            pltpu.VMEM(fourier.shape, BF16),
            pltpu.VMEM(filters.shape, BF16),
            pltpu.SemaphoreType.DMA((5,)),
        ],
        compiler_params=pltpu.CompilerParams(vmem_limit_bytes=24 << 20),
        name="log_mel",
    )(
        from_hbm(wave_pieces.reshape(slots, length)),
        from_hbm(piece_target.reshape(1, slots)),
        from_hbm(jnp.asarray(window)),
        from_hbm(jnp.asarray(fourier)),
        from_hbm(jnp.asarray(filters)),
    )
    if relative:
        received = [
            lax.ppermute(packed[d], "seq", [(i, i ^ d) for i in range(shards)])
            for d in range(shards - 1, 0, -1)
        ] + [packed[0]]
    else:
        blocks = packed[0].reshape(shards, capacity, payload)
        blocks = lax.all_to_all(blocks, "seq", split_axis=0, concat_axis=0, tiled=True)
        received = [blocks.reshape(slots, payload)]

    local_width = qkv_weight.shape[2]
    pairs = local_width // LANES
    gain = norm_gain.reshape(-1, LANES)
    rel_bias, gain, _ = lax.optimization_barrier((rel_bias, gain, packed[0]))
    entries = rel_bias.shape[1]
    qkv = jnp.transpose(qkv_weight, (1, 0, 2))
    bias, qkv = pl.pallas_call(
        prepare_kernel,
        out_shape=[
            pltpu.VMEM((pairs, n, 2 * ROWS, 3 * ROWS), F32),
            pltpu.VMEM(qkv.shape, BF16),
        ],
        in_specs=[in_hbm] * 3,
        out_specs=vmem(2),
        scratch_shapes=[
            pltpu.SMEM(utt_lengths.shape, jnp.int32),
            pltpu.VMEM(rel_bias.shape, F32),
            pltpu.VMEM((2 * pairs, entries + -entries % LANES), F32),
            pltpu.SemaphoreType.DMA((3,)),
        ],
        compiler_params=pltpu.CompilerParams(vmem_limit_bytes=8 << 20),
        cost_estimate=pl.CostEstimate(flops=1 << 31, bytes_accessed=8 << 20, transcendentals=0),
        name="prepare",
    )(from_hbm(utt_lengths), from_hbm(rel_bias), from_hbm(qkv))
    received, weight_got, bias_got, bias, qkv, gain = lax.optimization_barrier(
        (received, weight_got, bias_got, bias, qkv, gain)
    )
    own = pl.pallas_call(
        place_kernel,
        out_shape=jax.ShapeDtypeStruct((ROWS, STACK * MEL), BF16),
        in_specs=vmem(len(received)),
        out_specs=vmem(1)[0],
        compiler_params=pltpu.CompilerParams(vmem_limit_bytes=8 << 20),
        name="place",
    )(*received)
    conv = [sub_weight]
    for got in weight_got:
        got, _ = lax.optimization_barrier((got, own))
        conv += [got, lax.ppermute(got, "sub", [(0, 1), (1, 0)])]
    conv_bias = [line.reshape(-1, LANES) for line in [sub_bias] + bias_got]

    others = from_heads(own, n)
    width = qkv_weight.shape[0]
    qkv = in_vmem(qkv)
    limit = pltpu.CompilerParams(vmem_limit_bytes=16 << 20)
    limit = pltpu.CompilerParams(vmem_limit_bytes=16 << 20)
    *own_qkv, whole, whole_bias, whole_gain = pl.pallas_call(
        functools.partial(own_kernel, n),
        out_shape=[jax.ShapeDtypeStruct((1, ROWS, local_width), BF16)] * 3
        + [
            jax.ShapeDtypeStruct((sub_weight.shape[0], width), BF16),
            jax.ShapeDtypeStruct((1, width), F32),
            jax.ShapeDtypeStruct((1, width), F32),
        ],
        in_specs=vmem(1 + len(conv) + len(conv_bias) + 2),
        out_specs=vmem(6),
        scratch_shapes=[pltpu.VMEM((ROWS, width), BF16)],
        compiler_params=limit,
        cost_estimate=pl.CostEstimate(flops=1 << 20, bytes_accessed=1 << 20, transcendentals=0),
        name="own",
    )(own, *conv, *conv_bias, gain, qkv)
    weights = (whole, whole_bias, whole_gain, qkv)
    late, _ = lax.optimization_barrier((own, own_qkv[0]))
    rounds = [None] * n
    for r in reversed(range(n)):
        links = {}
        for g in range(groups):
            for k in range(shards - 1):
                for source, target in (
                    ((g, k, n - 1, 1), (g, k + 1, r, 0)),
                    ((g, k + 1, 0, 0), (g, k, n - 1 - r, 1)),
                ):
                    links[source] = target
        for source, target in list(links.items()):
            links.setdefault(target, source)
        for g in range(groups):
            for end in ((g, 0, 0, 0), (g, shards - 1, n - 1, 1)):
                beside = (*end[:3], 1 - end[3])
                if end not in links and beside not in links:
                    links.update({end: beside, beside: end})
        for place in itertools.product(range(groups), range(shards), range(n), range(cores)):
            links.setdefault(place, ((place[0] + 1) % groups, *place[1:]))
        assert len(set(links.values())) == len(links)
        sizes = (groups, shards, n, cores)
        flat = [tuple(int(np.ravel_multi_index(p, sizes)) for p in link) for link in links.items()]
        rounds[r] = lax.ppermute(late if r == 0 else own, ("groups", "seq", "head", "sub"), flat)
    *half_qkv, near_sent = pl.pallas_call(
        functools.partial(others_kernel, n),
        out_shape=[jax.ShapeDtypeStruct((n, ROWS, local_width), BF16)] * 3
        + [jax.ShapeDtypeStruct((2, ROWS, local_width), BF16)],
        in_specs=vmem(n + 2 + len(weights)),
        out_specs=vmem(4),
        scratch_shapes=[pltpu.VMEM(((n - 1) * ROWS, width), BF16)],
        compiler_params=limit,
        cost_estimate=pl.CostEstimate(flops=4 << 30, bytes_accessed=9 << 20, transcendentals=0),
        name="others",
    )(*own_qkv, *others, *weights)
    near = lax.ppermute(near_sent, "sub", [(0, 1), (1, 0)])
    far_context = pl.pallas_call(
        functools.partial(far_kernel, n),
        out_shape=jax.ShapeDtypeStruct((ROWS, local_width), BF16),
        in_specs=vmem(3 + n + len(weights) + 1),
        out_specs=vmem(1)[0],
        scratch_shapes=[
            pltpu.VMEM((ROWS, width), BF16),
            pltpu.VMEM((ROWS, local_width), BF16),
            pltpu.VMEM((ROWS, local_width), BF16),
        ],
        compiler_params=limit,
        cost_estimate=pl.CostEstimate(flops=16 << 30, bytes_accessed=9 << 20, transcendentals=0),
        name="far",
    )(*half_qkv, *rounds[::-1], *weights, in_vmem(bias))
    return pl.pallas_call(
        functools.partial(near_kernel, n),
        out_shape=jax.ShapeDtypeStruct((n * CH, local_width), BF16),
        in_specs=vmem(6),
        out_specs=in_hbm,
        scratch_shapes=[
            pltpu.VMEM((n * CH, local_width), BF16),
            pltpu.SemaphoreType.DMA((pairs,)),
        ],
        compiler_params=limit,
        name="near",
    )(*half_qkv, near, far_context, in_vmem(bias))


def solution(mesh):
    placed = (
        P(("groups", "seq"), "head", "sub", None, None),
        P(("groups", "seq"), "head", "sub", None),
        P("groups"),
        P(None, "head"),
        P("head"),
        P(),
        P(None, None, "head"),
        P("head", None),
    )
    return jax.shard_map(
        local,
        mesh=mesh,
        in_specs=placed,
        out_specs=P(("groups", "seq", "sub"), "head"),
        check_vma=False,
    )
```

```python
import functools
import itertools
import math

import jax
import jax.numpy as jnp
import ml_dtypes
import numpy as np
from jax import lax
from jax.experimental import pallas as pl
from jax.experimental.pallas import tpu as pltpu
from jax.sharding import PartitionSpec as P

HDIM = 64
MEL = 128
NFFT = 512
HOP = 160
FP = 17
CH = 136
PE = 32

SAMPLE_RATE = 16000.0
EPSILON = 1e-05
MASKED = -1e30

LANES = 128
PIECE_BITS = 5
ROWS = 144
GROUP = 4
STACK = 4
MEL_WIDTH = FP * MEL
BF16 = jnp.bfloat16
F32 = jnp.float32


def split_bf16(values):
    high = values.astype(ml_dtypes.bfloat16)
    low = (values - high.astype(np.float64)).astype(ml_dtypes.bfloat16)
    return np.stack([high, low])


def fourier_tables():
    n, bins = np.arange(NFFT // 2)[:, None], NFFT // 2

    def phase(k):
        return 2.0 * np.pi * ((n * k[None, :]) % NFFT) / NFFT

    even, odd = np.arange(0, bins, 2), np.arange(1, bins, 2)
    sine = np.sin(phase(even))
    sine[:, 0] = np.cos(phase(np.array([bins])))[:, 0]
    return np.stack(
        [
            split_bf16(np.concatenate([np.cos(phase(even)), sine], axis=1)),
            split_bf16(np.concatenate([np.cos(phase(odd)), np.sin(phase(odd))], axis=1)),
        ]
    )


def window_halves():
    window = 0.5 - 0.5 * np.cos(2.0 * np.pi * np.arange(NFFT) / NFFT)
    return window.reshape(2, NFFT // 2).astype(np.float32)


def mel_tables():
    bins = NFFT // 2
    highest = 2595.0 * math.log10(1.0 + SAMPLE_RATE / 2.0 / 700.0)
    points = np.arange(MEL + 2) * (highest / (MEL + 1))
    hertz = 700.0 * (10.0 ** (points / 2595.0) - 1.0)
    centres = np.arange(bins + 1) * (SAMPLE_RATE / NFFT)
    rising = (centres[:, None] - hertz[None, :-2]) / (hertz[1:-1] - hertz[:-2])[None, :]
    falling = (hertz[None, 2:] - centres[:, None]) / (hertz[2:] - hertz[1:-1])[None, :]
    filters = np.maximum(0.0, np.minimum(rising, falling))
    filters = [filters[0:bins:2], filters[1:bins:2], filters[bins:], np.zeros((15, MEL))]
    high, low = split_bf16(np.concatenate(filters, axis=0))
    return np.concatenate([high, low], axis=1)


def dot(a, b):
    return jnp.dot(a, b, preferred_element_type=F32)


def iota(shape, dim):
    return lax.broadcasted_iota(jnp.int32, shape, dim)


def mel_kernel(shards, capacity, relative, *refs):
    sources, outs = refs[:5], refs[5:-6]
    targets, sems = refs[-6:-1], refs[-1]
    x_ref, target_ref, window_ref, fourier_ref, mel_ref = targets
    slots = x_ref.shape[0]
    pairs = zip(sources, targets)
    copies = [pltpu.make_async_copy(*pair, sems.at[k]) for k, pair in enumerate(pairs)]
    for copy in copies:
        copy.start()
    copies[1].wait()
    target = target_ref[...]
    owner = lax.shift_right_arithmetic(target, PIECE_BITS)
    place = jnp.where(target < 0, 0, (target & (PE - 1)) + 1).astype(F32)
    row, col = iota((slots, slots), 0), iota((slots, slots), 1)
    diagonal = row == col
    owner_col = jnp.sum(jnp.where(diagonal, owner, 0), axis=1, keepdims=True)
    place_col = jnp.sum(jnp.where(diagonal, place, 0.0), axis=1, keepdims=True)
    rank = jnp.sum(((owner_col == owner) & (row < col)).astype(jnp.int32), axis=0, keepdims=True)
    chosen = row // capacity
    if relative:
        chosen = chosen ^ lax.axis_index("seq")
    pick = ((chosen == owner) & (row % capacity == rank)).astype(F32).astype(BF16)
    marks = jnp.broadcast_to(place_col, (slots, LANES)).astype(BF16)

    copies[0].wait()
    copies[2].wait()
    x = x_ref[...]
    frames = [None] * FP
    half, bins = NFFT // 2, NFFT // 4
    rising, falling = window_ref[0:1, :], window_ref[1:2, :]
    later = iota((1, bins), 1) > 0
    for phase in range(4):
        shift = phase * (HOP % LANES)
        moved = x if phase == 0 else pltpu.roll(x, x.shape[1] - shift, 1)
        members = list(range(phase, FP, 4))
        sums, differences = [], []
        for f in members:
            start = HOP * f - shift
            left = moved[:, start : start + half] * rising
            right = moved[:, start + half : start + NFFT] * falling
            sums.append(left + right)
            differences.append(left - right)
        squares = []
        for k, parts in enumerate((sums, differences)):
            values = jnp.concatenate(parts, axis=0)
            high = values.astype(BF16)
            low = (values - high.astype(F32)).astype(BF16)
            if phase == 0 and k == 0:
                copies[3].wait()
            table_high, table_low = fourier_ref[k, 0], fourier_ref[k, 1]
            spectra = dot(
                jnp.concatenate([high, low, high], axis=1),
                jnp.concatenate([table_high, table_high, table_low], axis=0),
            )
            squares.append(spectra * spectra)
        if phase == 0:
            copies[4].wait()
            filters = mel_ref[:half, :]
            last_row = mel_ref[half:, :].astype(F32)
            last_row = last_row[:1, :MEL] + last_row[:1, MEL:]
        even, odd = squares
        last = even[:, bins : bins + 1] * last_row
        even = even[:, :bins] + jnp.where(later, even[:, bins:], 0.0)
        power = jnp.concatenate([even, odd[:, :bins] + odd[:, bins:]], axis=1)
        power_high = power.astype(BF16)
        power_low = (power - power_high.astype(F32)).astype(BF16)
        both = dot(
            jnp.concatenate([power_high, power_low], axis=1),
            jnp.concatenate([filters, filters], axis=0),
        )
        energy = both[:, :MEL] + both[:, MEL:] + last
        log_mel = jnp.log(1.0 + energy).astype(BF16)
        for k, f in enumerate(members):
            frames[f] = log_mel[k * slots : (k + 1) * slots]
    packed = dot(pick, jnp.concatenate(frames + [marks], axis=1)).astype(BF16)
    count = slots // len(outs)
    for d, out in enumerate(outs):
        out[...] = packed[d * count : (d + 1) * count]


def token_rows(pieces):
    groups = PE // GROUP
    rows = []
    for i in range(FP):
        cells = []
        for j in range(STACK):
            q, f = divmod(STACK * i + j, FP)
            cells.append(pieces[q * groups : (q + 1) * groups, f * MEL : (f + 1) * MEL])
        rows.append(jnp.concatenate(cells, axis=1))
    rows.append(jnp.zeros((ROWS - CH, STACK * MEL), F32))
    mixed = jnp.concatenate(rows, axis=0).astype(BF16)
    row, col = iota((ROWS, ROWS), 0), iota((ROWS, ROWS), 1)
    token = (col % groups) * FP + col // groups
    order = ((row == token) & (col < CH)).astype(F32).astype(BF16)
    return dot(order, mixed).astype(BF16)


def place_kernel(*refs):
    parts, out = refs[:-1], refs[-1]
    rows = jnp.concatenate([part[...] for part in parts], axis=0)
    slots = rows.shape[0]
    mark = rows[:, MEL_WIDTH : MEL_WIDTH + LANES].astype(F32)[:, :1]
    row, col = iota((slots, slots), 0), iota((slots, slots), 1)
    mark = jnp.sum(jnp.where(row == col, mark, 0.0), axis=0, keepdims=True)
    at = iota((PE, slots), 0)
    groups = PE // GROUP
    wanted = (at % groups) * GROUP + at // groups + 1
    pick = (wanted.astype(F32) == mark).astype(F32).astype(BF16)
    out[...] = token_rows(dot(pick, rows[:, :MEL_WIDTH]))


def prepare_kernel(
    lengths_hbm, table_hbm, qkv_hbm, out_ref, qkv_ref, lengths_ref, table_ref, flipped, sems
):
    copies = [
        pltpu.make_async_copy(lengths_hbm, lengths_ref, sems.at[0]),
        pltpu.make_async_copy(table_hbm, table_ref, sems.at[1]),
        pltpu.make_async_copy(qkv_hbm, qkv_ref, sems.at[2]),
    ]
    for copy in copies:
        copy.start()
    copies[0].wait()
    copies[1].wait()
    pairs, blocks = out_ref.shape[:2]
    half = blocks * CH
    first = (lax.axis_index("seq") * lax.axis_size("sub") + lax.axis_index("sub")) * half
    total = lax.axis_size("seq") * lax.axis_size("sub") * half
    lane, row = iota((1, 3 * ROWS), 1), iota((ROWS, 1), 0)
    orders = ((0, 1, 2), (2, 0, 1))
    slot = lane // ROWS
    key_place = lane - slot * ROWS
    masks = []
    for c in range(blocks):
        order = orders[1 if c == blocks - 1 else 0]
        key_block = jnp.where(slot == 0, order[0], jnp.where(slot == 1, order[1], order[2]))
        query = first + c * CH + row
        key = first + (c - 1) * CH + key_block * CH + key_place
        query_utt, key_utt = jnp.zeros_like(query), jnp.zeros_like(key)
        end = jnp.int32(0)
        for r in range(lengths_ref.shape[0]):
            end = end + lengths_ref[r]
            query_utt = query_utt + (query >= end).astype(jnp.int32)
            key_utt = key_utt + (key >= end).astype(jnp.int32)
        inside = (key >= 0) & (key < total) & (key_place < CH)
        key_utt = jnp.where(inside, key_utt, -1)
        masks.append(jnp.where(query_utt == key_utt, 0.0, MASKED))
    heads, entries = table_ref.shape
    width = flipped.shape[1]
    mirror = iota((entries, width), 0) + iota((entries, width), 1) == entries - 1
    mirror = mirror.astype(F32).astype(BF16)
    rest, lines = table_ref[...], 0.0
    for _ in range(3):
        part = rest.astype(BF16)
        rest = rest - part.astype(F32)
        lines = lines + dot(part, mirror)
    flipped[...] = lines

    def one_head(head, side):
        line = jnp.broadcast_to(flipped[pl.ds(head, 1), :], (ROWS, width))
        biases = []
        for order in orders:
            turned = [
                pltpu.roll(
                    line, (ROWS * at - CH * b - (CH - 1)) % width, 1, stride=1, stride_axis=0
                )[:, : 3 * ROWS]
                for at, b in enumerate(order)
            ]
            biases.append(
                jnp.where(slot == 0, turned[0], jnp.where(slot == 1, turned[1], turned[2]))
            )
        for c in range(blocks):
            bias = biases[1 if c == blocks - 1 else 0]
            out_ref[head // 2, c, side * ROWS : (side + 1) * ROWS, :] = bias + masks[c]

    @pl.loop(0, pairs)
    def _(pair):
        one_head(2 * pair, 0)
        one_head(2 * pair + 1, 1)

    copies[2].wait()


def normalize(tokens, conv, conv_bias, gain, out):
    summed = dot(tokens, conv[...]) + conv_bias[...]
    half = 0.5 * summed
    features = (half + half * jnp.tanh(half)).astype(BF16).astype(F32)
    scale = 1.0 / features.shape[1]
    centred = features - jnp.sum(features, axis=1, keepdims=True) * scale
    variance = jnp.sum(centred * centred, axis=1, keepdims=True) * scale
    out[...] = (centred * lax.rsqrt(variance + EPSILON) * gain[...]).astype(BF16)


def own_kernel(n, *refs):
    pieces, parts, refs = refs[0], refs[1 : 2 * n], refs[2 * n :]
    bias_parts, gain_rows, refs = refs[:n], refs[n], refs[n + 1 :]
    qkv, q_out, k_out, v_out, conv, conv_bias, gain, normed = refs
    me, core = lax.axis_index("head"), lax.axis_index("sub")
    depth = parts[0].shape[1]
    for d in range(n):
        start = pl.multiple_of(lax.rem(me + d, n) * depth, depth)
        at = pl.ds(start, depth)
        lines = bias_parts[d][...].astype(F32)
        for k in range(depth // LANES):
            conv_bias[:, pl.ds(start + k * LANES, LANES)] = lines[k : k + 1]
        if d == 0:
            conv[:, at] = parts[0][...]
        else:
            got, swapped = parts[2 * d - 1 : 2 * d + 1]

            @pl.when(core == 0)
            def _(got=got, at=at):
                conv[:, at] = got[...]

            @pl.when(core == 1)
            def _(swapped=swapped, at=at):
                conv[:, at] = swapped[...]

    for k in range(gain_rows.shape[0]):
        gain[:, k * LANES : (k + 1) * LANES] = gain_rows[k : k + 1, :]
    normalize(pieces[...], conv, conv_bias, gain, normed)
    for p, out in enumerate((q_out, k_out, v_out)):
        out[0] = dot(normed[...], qkv[p]).astype(BF16)


def others_kernel(n, *refs):
    own, pieces = refs[:3], refs[3 : n + 2]
    conv, conv_bias, gain, qkv, *outs, sent, normed = refs[n + 2 :]
    me, core = lax.axis_index("head"), lax.axis_index("sub")
    tokens = jnp.concatenate([piece[...] for piece in pieces], axis=0)
    normalize(tokens, conv, conv_bias, gain, normed)
    wanted = jnp.where(core == 0, n - 1, 0)
    for p, (source, out) in enumerate(zip(own, outs)):
        out[me] = source[0]
        got = dot(normed[...], qkv[p]).astype(BF16)
        for d in range(1, n):
            out[lax.rem(me + d, n)] = got[(d - 1) * ROWS : d * ROWS]
        if p > 0:
            sent[p - 1] = out[wanted]


def attend(q, k, v, bias):
    low_lanes = iota((ROWS, LANES), 1) < HDIM
    q = q * jnp.asarray(1.0 / math.sqrt(HDIM), BF16)
    zero = jnp.zeros_like(q)
    q = jnp.concatenate([jnp.where(low_lanes, q, zero), jnp.where(low_lanes, zero, q)], axis=0)
    scores = lax.dot_general(q, k, (((1,), (1,)), ((), ())), preferred_element_type=F32) + bias
    weights = jnp.exp(scores - jnp.max(scores, axis=1, keepdims=True)).astype(BF16)
    summed = dot(weights, jnp.concatenate([v, jnp.ones_like(v)], axis=1))
    context = summed[:, :LANES] * (1.0 / summed[:, LANES:])
    return jnp.where(low_lanes, context[:ROWS], context[ROWS:])


def edge_context(pair, block, halo_keys, halo_values, first, queries, keys, values, bias):
    at = slice(pair * LANES, (pair + 1) * LANES)
    return attend(
        queries[block, :, at],
        jnp.concatenate([halo_keys[:, at], keys[first, :, at], keys[first + 1, :, at]], axis=0),
        jnp.concatenate(
            [halo_values[:, at], values[first, :, at], values[first + 1, :, at]], axis=0
        ),
        bias[pair, block],
    )


def far_kernel(n, *refs):
    (queries, keys, values), rounds, refs = refs[:3], refs[3 : n + 3], refs[n + 3 :]
    conv, conv_bias, gain, qkv, bias, out, normed, far_keys, far_values = refs
    me, core = lax.axis_index("head"), lax.axis_index("sub")
    far, turn = rounds[0][...], jnp.where(core == 0, n - 1 - me, me)
    for r in range(1, n):
        far = jnp.where(turn == r, rounds[r][...], far)
    normalize(far, conv, conv_bias, gain, normed)
    far_keys[...] = dot(normed[...], qkv[1]).astype(BF16)
    far_values[...] = dot(normed[...], qkv[2]).astype(BF16)
    block, first = jnp.where(core == 0, 0, n - 1), jnp.where(core == 0, 0, n - 2)
    for pair in range(qkv.shape[2] // LANES):
        context = edge_context(
            pair, block, far_keys, far_values, first, queries, keys, values, bias
        )
        out[:, pair * LANES : (pair + 1) * LANES] = context.astype(BF16)


def near_kernel(n, *refs):
    queries, keys, values, near, far_context, bias, out_hbm, out, sems = refs
    core = lax.axis_index("sub")
    copies = []
    block, first = jnp.where(core == 0, n - 1, 0), jnp.where(core == 0, n - 2, 0)
    for pair in range(queries.shape[2] // LANES):
        at = slice(pair * LANES, (pair + 1) * LANES)
        context = edge_context(
            pair, block, near.at[0], near.at[1], first, queries, keys, values, bias
        )[:CH]
        middle = [
            attend(
                queries[c, :, at],
                keys[c - 1 : c + 2, :, at].reshape(3 * ROWS, LANES),
                values[c - 1 : c + 2, :, at].reshape(3 * ROWS, LANES),
                bias[pair, c],
            )[:CH]
            for c in range(1, n - 1)
        ]
        other = far_context[:, at].astype(F32)[:CH]
        out[:, at] = jnp.where(
            core == 0,
            jnp.concatenate([other] + middle + [context], axis=0),
            jnp.concatenate([context] + middle + [other], axis=0),
        ).astype(BF16)
        copies.append(pltpu.make_async_copy(out.at[:, at], out_hbm.at[:, at], sems.at[pair]))
        copies[-1].start()
    for copy in copies:
        copy.wait()


def vmem(count):
    return [pl.BlockSpec(memory_space=pltpu.VMEM)] * count


def from_hbm(array):
    return pltpu.with_memory_space_constraint(array, pltpu.HBM)


def in_vmem(array):
    return pltpu.with_memory_space_constraint(array, pltpu.VMEM)


def from_heads(block, n):
    return [lax.ppermute(block, "head", [((i + d) % n, i) for i in range(n)]) for d in range(1, n)]


def local(
    wave_pieces, piece_target, utt_lengths, sub_weight, sub_bias, norm_gain, qkv_weight, rel_bias
):
    shards, n, cores = lax.axis_size("seq"), lax.axis_size("head"), lax.axis_size("sub")
    assert cores == 2
    slots, length = wave_pieces.shape[3:]
    capacity = slots // shards
    relative = shards in (2, 4) and capacity % 16 == 0
    outs = shards if relative else 1
    payload = MEL_WIDTH + LANES
    fourier, filters, window = fourier_tables(), mel_tables(), window_halves()
    in_hbm = pl.BlockSpec(memory_space=pltpu.HBM)
    groups = lax.axis_size("groups")
    weight_got, bias_got = [], from_heads(sub_bias, n)
    for d in range(1, n):
        links = []
        for g in range(groups):
            for h in range(n):
                at = (g * n + h) * cores
                links.append(((g * n + (h + d) % n) * cores, at))
                links.append((((g + 1) % groups * n + h) * cores + 1, at + 1))
        weight_got.append(lax.ppermute(sub_weight, ("groups", "head", "sub"), links))
    packed = pl.pallas_call(
        functools.partial(mel_kernel, shards, capacity, relative),
        out_shape=[jax.ShapeDtypeStruct((slots // outs, payload), BF16)] * outs,
        in_specs=[in_hbm] * 5,
        out_specs=vmem(outs),
        scratch_shapes=[
            pltpu.VMEM((slots, length), F32),
            pltpu.VMEM((1, slots), jnp.int32),
            pltpu.VMEM(window.shape, F32),
            pltpu.VMEM(fourier.shape, BF16),
            pltpu.VMEM(filters.shape, BF16),
            pltpu.SemaphoreType.DMA((5,)),
        ],
        compiler_params=pltpu.CompilerParams(vmem_limit_bytes=24 << 20),
        name="log_mel",
    )(
        from_hbm(wave_pieces.reshape(slots, length)),
        from_hbm(piece_target.reshape(1, slots)),
        from_hbm(jnp.asarray(window)),
        from_hbm(jnp.asarray(fourier)),
        from_hbm(jnp.asarray(filters)),
    )
    if relative:
        received = [
            lax.ppermute(packed[d], "seq", [(i, i ^ d) for i in range(shards)])
            for d in range(shards - 1, 0, -1)
        ] + [packed[0]]
    else:
        blocks = packed[0].reshape(shards, capacity, payload)
        blocks = lax.all_to_all(blocks, "seq", split_axis=0, concat_axis=0, tiled=True)
        received = [blocks.reshape(slots, payload)]

    local_width = qkv_weight.shape[2]
    pairs = local_width // LANES
    gain = norm_gain.reshape(-1, LANES)
    rel_bias, gain, _ = lax.optimization_barrier((rel_bias, gain, packed[0]))
    entries = rel_bias.shape[1]
    qkv = jnp.transpose(qkv_weight, (1, 0, 2))
    bias, qkv = pl.pallas_call(
        prepare_kernel,
        out_shape=[
            pltpu.VMEM((pairs, n, 2 * ROWS, 3 * ROWS), F32),
            pltpu.VMEM(qkv.shape, BF16),
        ],
        in_specs=[in_hbm] * 3,
        out_specs=vmem(2),
        scratch_shapes=[
            pltpu.SMEM(utt_lengths.shape, jnp.int32),
            pltpu.VMEM(rel_bias.shape, F32),
            pltpu.VMEM((2 * pairs, entries + -entries % LANES), F32),
            pltpu.SemaphoreType.DMA((3,)),
        ],
        compiler_params=pltpu.CompilerParams(vmem_limit_bytes=8 << 20),
        cost_estimate=pl.CostEstimate(flops=1 << 31, bytes_accessed=8 << 20, transcendentals=0),
        name="prepare",
    )(from_hbm(utt_lengths), from_hbm(rel_bias), from_hbm(qkv))
    received, weight_got, bias_got, bias, qkv, gain = lax.optimization_barrier(
        (received, weight_got, bias_got, bias, qkv, gain)
    )
    own = pl.pallas_call(
        place_kernel,
        out_shape=jax.ShapeDtypeStruct((ROWS, STACK * MEL), BF16),
        in_specs=vmem(len(received)),
        out_specs=vmem(1)[0],
        compiler_params=pltpu.CompilerParams(vmem_limit_bytes=8 << 20),
        name="place",
    )(*received)
    conv = [sub_weight]
    for got in weight_got:
        conv += [got, lax.ppermute(got, "sub", [(0, 1), (1, 0)])]
    conv_bias = [line.reshape(-1, LANES) for line in [sub_bias] + bias_got]

    others = from_heads(own, n)
    width = qkv_weight.shape[0]
    qkv = in_vmem(qkv)
    limit = pltpu.CompilerParams(vmem_limit_bytes=16 << 20)
    limit = pltpu.CompilerParams(vmem_limit_bytes=16 << 20)
    *own_qkv, whole, whole_bias, whole_gain = pl.pallas_call(
        functools.partial(own_kernel, n),
        out_shape=[jax.ShapeDtypeStruct((1, ROWS, local_width), BF16)] * 3
        + [
            jax.ShapeDtypeStruct((sub_weight.shape[0], width), BF16),
            jax.ShapeDtypeStruct((1, width), F32),
            jax.ShapeDtypeStruct((1, width), F32),
        ],
        in_specs=vmem(1 + len(conv) + len(conv_bias) + 2),
        out_specs=vmem(6),
        scratch_shapes=[pltpu.VMEM((ROWS, width), BF16)],
        compiler_params=limit,
        cost_estimate=pl.CostEstimate(flops=1 << 20, bytes_accessed=1 << 20, transcendentals=0),
        name="own",
    )(own, *conv, *conv_bias, gain, qkv)
    weights = (whole, whole_bias, whole_gain, qkv)
    late, _ = lax.optimization_barrier((own, own_qkv[0]))
    rounds = [None] * n
    for r in reversed(range(n)):
        links = {}
        for g in range(groups):
            for k in range(shards - 1):
                for source, target in (
                    ((g, k, n - 1, 1), (g, k + 1, r, 0)),
                    ((g, k + 1, 0, 0), (g, k, n - 1 - r, 1)),
                ):
                    links[source] = target
        for source, target in list(links.items()):
            links.setdefault(target, source)
        for g in range(groups):
            for end in ((g, 0, 0, 0), (g, shards - 1, n - 1, 1)):
                beside = (*end[:3], 1 - end[3])
                if end not in links and beside not in links:
                    links.update({end: beside, beside: end})
        for place in itertools.product(range(groups), range(shards), range(n), range(cores)):
            links.setdefault(place, ((place[0] + 1) % groups, *place[1:]))
        assert len(set(links.values())) == len(links)
        sizes = (groups, shards, n, cores)
        flat = [tuple(int(np.ravel_multi_index(p, sizes)) for p in link) for link in links.items()]
        rounds[r] = lax.ppermute(late if r == 0 else own, ("groups", "seq", "head", "sub"), flat)
    *half_qkv, near_sent = pl.pallas_call(
        functools.partial(others_kernel, n),
        out_shape=[jax.ShapeDtypeStruct((n, ROWS, local_width), BF16)] * 3
        + [jax.ShapeDtypeStruct((2, ROWS, local_width), BF16)],
        in_specs=vmem(n + 2 + len(weights)),
        out_specs=vmem(4),
        scratch_shapes=[pltpu.VMEM(((n - 1) * ROWS, width), BF16)],
        compiler_params=limit,
        cost_estimate=pl.CostEstimate(flops=4 << 30, bytes_accessed=9 << 20, transcendentals=0),
        name="others",
    )(*own_qkv, *others, *weights)
    near = lax.ppermute(near_sent, "sub", [(0, 1), (1, 0)])
    far_context = pl.pallas_call(
        functools.partial(far_kernel, n),
        out_shape=jax.ShapeDtypeStruct((ROWS, local_width), BF16),
        in_specs=vmem(3 + n + len(weights) + 1),
        out_specs=vmem(1)[0],
        scratch_shapes=[
            pltpu.VMEM((ROWS, width), BF16),
            pltpu.VMEM((ROWS, local_width), BF16),
            pltpu.VMEM((ROWS, local_width), BF16),
        ],
        compiler_params=limit,
        cost_estimate=pl.CostEstimate(flops=16 << 30, bytes_accessed=9 << 20, transcendentals=0),
        name="far",
    )(*half_qkv, *rounds[::-1], *weights, in_vmem(bias))
    return pl.pallas_call(
        functools.partial(near_kernel, n),
        out_shape=jax.ShapeDtypeStruct((n * CH, local_width), BF16),
        in_specs=vmem(6),
        out_specs=in_hbm,
        scratch_shapes=[
            pltpu.VMEM((n * CH, local_width), BF16),
            pltpu.SemaphoreType.DMA((pairs,)),
        ],
        compiler_params=limit,
        name="near",
    )(*half_qkv, near, far_context, in_vmem(bias))


def solution(mesh):
    placed = (
        P(("groups", "seq"), "head", "sub", None, None),
        P(("groups", "seq"), "head", "sub", None),
        P("groups"),
        P(None, "head"),
        P("head"),
        P(),
        P(None, None, "head"),
        P("head", None),
    )
    return jax.shard_map(
        local,
        mesh=mesh,
        in_specs=placed,
        out_specs=P(("groups", "seq", "sub"), "head"),
        check_vma=False,
    )
```
